32 devices in a mesh: dp: 8 (over z, y), tensor: 4 (over x, core).
Axes of the slice: x: 2, y: 2, z: 4, core: 2. Of those that a mesh axis runs over, the one named last changes fastest.
Arguments:
- tokens: bfloat16 [8192, 2048], P('dp'), may hold values from -6 to 6
- seg_ids: int32 [8192], P('dp'), may hold values from -1 to 1023, as said below
- cotangent: bfloat16 [8192, 2048], P('dp'), may hold values from -6 to 6
- attn_gain: float32 [2048], replicated, may hold values from 0.5 to 1.5
- w_query: bfloat16 [2048, 2048], P(None, 'tensor'), may hold values from -0.125 to 0.125
- w_key: bfloat16 [2048, 1024], P(None, 'tensor'), may hold values from -0.125 to 0.125
- w_value: bfloat16 [2048, 1024], P(None, 'tensor'), may hold values from -0.125 to 0.125
- w_out: bfloat16 [2048, 2048], P('tensor'), may hold values from -0.5 to 0.5
- mlp_gain: float32 [2048], replicated, may hold values from 0.5 to 1.5
- w_gate: bfloat16 [2048, 6144], P(None, 'tensor'), may hold values from -0.125 to 0.125
- w_up: bfloat16 [2048, 6144], P(None, 'tensor'), may hold values from -0.125 to 0.125
- w_down: bfloat16 [6144, 2048], P('tensor'), may hold values from -0.078125 to 0.078125
- query_gain: float32 [128], replicated, may hold values from 0.5 to 1.5
- key_gain: float32 [128], replicated, may hold values from 0.5 to 1.5
Outputs:
- mixed: bfloat16 [8192, 2048], P('dp')
- grad_tokens: bfloat16 [8192, 2048], P('dp')
- grad_attn_gain: float32 [2048], P('dp')
- grad_query: float32 [2048, 2048], P('dp', 'tensor')
- grad_key: float32 [2048, 1024], P('dp', 'tensor')
- grad_value: float32 [2048, 1024], P('dp', 'tensor')
- grad_out: float32 [2048, 2048], P('tensor', 'dp')
- grad_mlp_gain: float32 [2048], P('dp')
- grad_gate: float32 [2048, 6144], P('dp', 'tensor')
- grad_up: float32 [2048, 6144], P('dp', 'tensor')
- grad_down: float32 [6144, 2048], P('tensor', 'dp')
- grad_qgain: float32 [128], P('dp')
- grad_kgain: float32 [128], P('dp')
The draws below stay inside these ranges and needn't reach their ends.
Inputs may be any that keep to these rules, and one draw needn't show every extreme that they name: `seg_ids`: in each aligned block of 1024 slots (the slots of one index of dp) the live slots come first and padding (-1) fills the rest; a live slot holds the index in its block of its sequence's first slot, so ids never fall within a block. One block per draw is a single sequence of 1024 slots; the next block (the first one, if it is the last) is full, its last slot a sequence of one slot; every other block ends in padding.
All inputs are finite; a program needn't handle non-finite values.
Results may differ from the reference program's by a relative error of at most 0.02.
Values may be sent and summed in bfloat16 or wider, within the bound.
No kernel may reach another device: no remote copies, remote signals or barrier semaphores. Data moves between devices by JAX's collectives and lax.ppermute only.
A program may use at most 256 MiB of HBM per device.

```python
import jax
import jax.numpy as jnp
from jax import lax

D = 2048
HQ = 16
HK = 8
HD = 128
FF = 6144
TOK_DEV = 1024
TOKENS = 8192
N_DP = 8


def draw_seg_ids(key, part):
    key = jax.random.fold_in(key, 11)
    first, second, third = jax.random.split(key, 3)
    index = jnp.arange(TOK_DEV, dtype=jnp.int32)[None, :]
    device = jnp.arange(N_DP, dtype=jnp.int32)[:, None]
    whole = jax.random.randint(first, (), 0, N_DP)
    filled = (whole + 1) % N_DP
    live = jax.random.randint(second, (N_DP, 1), TOK_DEV // 4, TOK_DEV)
    live = jnp.where((device == whole) | (device == filled), TOK_DEV, live)
    begins = jax.random.randint(third, (N_DP, TOK_DEV), 0, TOK_DEV // 4) == 0
    begins = begins & (device != whole) | (index == 0) | (device == filled) & (index == TOK_DEV - 1)
    starts = lax.cummax(jnp.where(begins, index, 0), axis=1)
    seg = jnp.where(index < live, starts, -1)
    return seg.reshape(-1).astype(jnp.int32)


def block_scale(rng, extent, pieces, low, top_value):
    def one(position, shards_of):
        draws = jax.random.uniform(jax.random.fold_in(jax.random.fold_in(rng, 6), position), (shards_of,), jnp.float32, low / len(pieces), top_value / len(pieces))
        return jnp.repeat(jnp.exp(draws), extent[position] // shards_of).reshape((-1,) + (1,) * (len(extent) - position - 1))

    loudness = one(*pieces[0])
    for cut in pieces[1:]:
        loudness = loudness * one(*cut)
    return loudness


def gaussian(stream_key, shape, spread, most, shards=(), kind=jnp.bfloat16):
    entries = jax.random.normal(stream_key, shape, jnp.float32) * spread
    if len(shards) > 0:
        entries = block_scale(stream_key, shape, shards, -0.22, 0.18) * entries
    return jnp.clip(entries, min=-most, max=most).astype(kind)


def setup_inputs(seed: int = 0) -> dict:
    splits = jax.random.split(jax.random.key(seed), 15)
    tokens = gaussian(splits[0], (TOKENS, D), 1.0, 6.0, ((0, 8),))
    seg_ids = draw_seg_ids(jax.random.fold_in(splits[14], 71), 0)
    cotangent = gaussian(splits[2], (TOKENS, D), 1.0, 6.0, ((0, 8),))
    attn_gain = jnp.clip(1.0 + 0.1 * jax.random.normal(splits[3], (D,), jnp.float32), 0.5, 1.5)
    w_query = gaussian(splits[4], (D, HQ * HD), D ** -0.5, 0.125, ((1, 4),))
    w_key = gaussian(splits[5], (D, HK * HD), D ** -0.5, 0.125, ((1, 4),))
    w_value = gaussian(splits[6], (D, HK * HD), D ** -0.5, 0.125, ((1, 4),))
    w_out = gaussian(splits[7], (HQ * HD, D), (HQ * HD // 16) ** -0.5, 0.5, ((0, 4),))
    mlp_gain = jnp.clip(1.0 + 0.1 * jax.random.normal(splits[8], (D,), jnp.float32), 0.5, 1.5)
    w_gate = gaussian(splits[9], (D, FF), D ** -0.5, 0.125, ((1, 4),))
    w_up = gaussian(splits[10], (D, FF), D ** -0.5, 0.125, ((1, 4),))
    w_down = gaussian(splits[11], (FF, D), FF ** -0.5, 0.078125, ((0, 4),))
    query_gain = jnp.clip(1.0 + 0.1 * jax.random.normal(splits[12], (HD,), jnp.float32), 0.5, 1.5)
    key_gain = jnp.clip(1.0 + 0.1 * jax.random.normal(splits[13], (HD,), jnp.float32), 0.5, 1.5)
    return dict(tokens=tokens, seg_ids=seg_ids, cotangent=cotangent, attn_gain=attn_gain, w_query=w_query, w_key=w_key, w_value=w_value, w_out=w_out, mlp_gain=mlp_gain, w_gate=w_gate, w_up=w_up, w_down=w_down, query_gain=query_gain, key_gain=key_gain)


EPS = 1e-06
THETA = 1000000.0

@jax.custom_vjp
def low(v):
    return lax.optimization_barrier(v.astype(jnp.bfloat16)).astype(jnp.float32)

@jax.custom_vjp
def low_back(v):
    return v

def low_keep(v):
    return (low(v), None)

def low_pass(kept, grad):
    return (grad,)

def back_keep(v):
    return (v, None)

def back_low(kept, grad):
    return (low(grad),)
low.defvjp(low_keep, low_pass)
low_back.defvjp(back_keep, back_low)

def matmul(left, right):
    return jnp.dot(left, right, precision=lax.Precision.HIGHEST)

def rms(value, gain):
    return value * lax.rsqrt(lax.optimization_barrier(jnp.mean(value * value, -1, keepdims=True)) + EPS) * gain

def rotate(value, cosine, sine):
    half = value.shape[-1] // 2
    turned = jnp.concatenate([-value[..., half:], value[..., :half]], -1)
    return value * cosine + turned * sine

def angles(seg_ids):
    blocks = seg_ids.reshape(N_DP, TOK_DEV)
    index = jnp.arange(TOK_DEV, dtype=jnp.int32)[None, :]
    place = jnp.where(blocks >= 0, index - blocks, index).reshape(-1).astype(jnp.float32)
    freq = THETA ** (-(jnp.arange(HD // 2, dtype=jnp.float32) * 2.0) / HD)
    turn = place[:, None] * freq[None, :]
    turn = jnp.concatenate([turn, turn], -1)[:, None, :]
    return (jnp.cos(turn), jnp.sin(turn))

def attend(block):
    queries, keys, values, ids = block
    group = HQ // HK
    query_g = queries.reshape(TOK_DEV, HK, group, HD)
    scores = jnp.einsum('qgrd,kgd->grqk', query_g, keys, precision=lax.Precision.HIGHEST)
    scores = low_back(scores)
    index = jnp.arange(TOK_DEV, dtype=jnp.int32)
    allowed = (ids[:, None] == ids[None, :]) & (index[None, :] <= index[:, None])
    scores = jnp.where(allowed, scores, -1e+30)
    expo = jnp.exp(scores - lax.optimization_barrier(jnp.max(scores, -1, keepdims=True)))
    probs = low(expo / lax.optimization_barrier(jnp.sum(expo, -1, keepdims=True)))
    attended = jnp.einsum('grqk,kgd->qgrd', probs, values, precision=lax.Precision.HIGHEST)
    return attended.reshape(TOK_DEV, HQ * HD)

def forward(x, attn_gain, w_query, w_key, w_value, w_out, mlp_gain, w_gate, w_up, w_down, query_gain, key_gain, seg_ids):
    normed = low(rms(x, attn_gain))
    q_lin = low_back(matmul(normed, w_query)).reshape(TOKENS, HQ, HD)
    k_lin = low_back(matmul(normed, w_key)).reshape(TOKENS, HK, HD)
    values = low(low_back(matmul(normed, w_value))).reshape(TOKENS, HK, HD)
    cosine, sine = angles(seg_ids)
    queries = low(low_back(rotate(rms(q_lin, query_gain), cosine, sine) * HD ** (-0.5)))
    keys = low(low_back(rotate(rms(k_lin, key_gain), cosine, sine)))
    attended = lax.map(jax.checkpoint(attend), (queries.reshape(N_DP, TOK_DEV, HQ, HD), keys.reshape(N_DP, TOK_DEV, HK, HD), values.reshape(N_DP, TOK_DEV, HK, HD), seg_ids.reshape(N_DP, TOK_DEV)))
    attended = low(low_back(attended.reshape(TOKENS, HQ * HD)))
    resid = x + low_back(matmul(attended, w_out))
    inner = low(rms(resid, mlp_gain))
    gate = low_back(matmul(inner, w_gate))
    up = low_back(matmul(inner, w_up))
    hidden = low(jax.nn.silu(gate) * up)
    return resid + low_back(matmul(hidden, w_down))

def reference(tokens, seg_ids, cotangent, attn_gain, w_query, w_key, w_value, w_out, mlp_gain, w_gate, w_up, w_down, query_gain, key_gain):
    primals = (tokens.astype(jnp.float32), attn_gain.astype(jnp.float32), w_query.astype(jnp.float32), w_key.astype(jnp.float32), w_value.astype(jnp.float32), w_out.astype(jnp.float32), mlp_gain.astype(jnp.float32), w_gate.astype(jnp.float32), w_up.astype(jnp.float32), w_down.astype(jnp.float32), query_gain.astype(jnp.float32), key_gain.astype(jnp.float32))

    def closed(*args):
        return forward(*args, seg_ids)
    mixed, pull = jax.vjp(closed, *primals)
    live = (seg_ids >= 0).astype(jnp.float32)[:, None]
    grads = pull(cotangent.astype(jnp.float32) * live)
    return (mixed.astype(jnp.bfloat16), grads[0].astype(jnp.bfloat16), grads[1], grads[2], grads[3], grads[4], grads[5], grads[6], grads[7], grads[8], grads[9], grads[10], grads[11])
```

```python
import functools

import jax
import jax.numpy as jnp
import numpy as np
from jax import lax
from jax.sharding import PartitionSpec as P

EPS = 1e-06
THETA = 1000000.0
CORE_SWAP = ((0, 1), (1, 0), (2, 3), (3, 2))
CHIP_SWAP = ((0, 2), (1, 3), (2, 0), (3, 1))


def lowered(value):
    return lax.optimization_barrier(value.astype(jnp.bfloat16)).astype(jnp.float32)


def norm_fwd(value):
    factor = lax.rsqrt(jnp.mean(value * value, -1, keepdims=True) + EPS)
    return (value * factor, factor)


def norm_back(d_hat, v_hat, factor):
    return factor * (d_hat - v_hat * jnp.mean(d_hat * v_hat, -1, keepdims=True))


def rotate(value, cosine, sine):
    half = value.shape[-1] // 2
    turned = jnp.concatenate([-value[..., half:], value[..., :half]], -1)
    return value * cosine + turned * sine


def rotate_back(grad, cosine, sine):
    half = grad.shape[-1] // 2
    weighted = grad * sine
    turned = jnp.concatenate([-weighted[..., half:], weighted[..., :half]], -1)
    return grad * cosine - turned


def inner_dot(left, right):
    return lax.dot_general(
        left, right, (((0,), (0,)), ((), ())), preferred_element_type=jnp.float32
    )


def outer_dot(left, right):
    return lax.dot_general(
        left, right, (((1,), (1,)), ((), ())), preferred_element_type=jnp.float32
    )


def to_core(value):
    return lax.ppermute(value, "tensor", CORE_SWAP)


def to_chip(value):
    return lax.ppermute(value, "tensor", CHIP_SWAP)


def ring_of(n):
    order = list(range(0, n, 2)) + [i for i in range(n - 1, 0, -1) if i % 2]
    place = [0] * n
    for spot, index in enumerate(order):
        place[index] = spot
    ahead = tuple((order[i], order[(i + 1) % n]) for i in range(n))
    back = tuple((b, a) for a, b in ahead)
    return order, place, ahead, back


def ring_scatter(n, part, dim):
    order, place, ahead, back = ring_of(n)
    spot = jnp.asarray(np.array(place, np.int32))[lax.axis_index("dp")]
    order = jnp.asarray(np.array(order, np.int32))
    size = part.shape[dim] // n
    other = 1 - dim
    wide = part.shape[other] // 2

    def piece(where, side):
        begin = [0, 0]
        extent = [0, 0]
        begin[dim] = order[where % n] * size
        extent[dim] = size
        begin[other] = side * wide
        extent[other] = wide
        return lax.dynamic_slice(part, begin, extent)

    held = [piece(spot - 1 + n, 0), piece(spot + 1, 1)]
    for step in range(n - 1):
        for side, pairs in ((0, ahead), (1, back)):
            came = lax.ppermute(held[side], "dp", pairs)
            where = spot + 2 * n - 2 - step if side == 0 else spot + 2 + step
            held[side] = came.astype(jnp.float32) + piece(where, side).astype(jnp.float32)
            if step < n - 2:
                held[side] = held[side].astype(jnp.bfloat16)
    return jnp.concatenate(held, other)


def all_sum_dp(n, value):
    step = 1
    while step < n:
        value = value + lax.ppermute(value, "dp", tuple((i, i ^ step) for i in range(n)))
        step *= 2
    return value


def on_device(
    n,
    tokens,
    seg_ids,
    cotangent,
    attn_gain,
    w_query,
    w_key,
    w_value,
    w_out,
    mlp_gain,
    w_gate,
    w_up,
    w_down,
    query_gain,
    key_gain,
):
    count = tokens.shape[0]
    half = count // 2
    head_size = query_gain.shape[0]
    q_count = w_query.shape[1] // head_size
    kv_count = w_key.shape[1] // head_size
    group = q_count // kv_count
    scale = head_size ** (-0.5)
    core = lax.axis_index("tensor") % 2
    scatter = functools.partial(ring_scatter, n)

    def mine(value):
        return lax.dynamic_slice_in_dim(value, core * half, half, 0)

    def other(value):
        return lax.dynamic_slice_in_dim(value, (1 - core) * half, half, 0)

    def ordered(first, second):
        return jnp.where(
            core == 0, jnp.concatenate([first, second], 0), jnp.concatenate([second, first], 0)
        )

    def summed(part_mine, part_other):
        near = part_mine + to_core(part_other.astype(jnp.bfloat16)).astype(jnp.float32)
        near = near.astype(jnp.bfloat16)
        far = to_chip(near)
        return near.astype(jnp.float32) + far.astype(jnp.float32)

    x_full = tokens.astype(jnp.float32)
    x_hat, r_x = norm_fwd(x_full)
    normed = (x_hat * attn_gain).astype(jnp.bfloat16)
    q_lin = jnp.dot(normed, w_query, preferred_element_type=jnp.float32).reshape(
        count, q_count, head_size
    )
    k_lin = jnp.dot(normed, w_key, preferred_element_type=jnp.float32).reshape(
        count, kv_count, head_size
    )
    values = (
        jnp.dot(normed, w_value, preferred_element_type=jnp.float32)
        .astype(jnp.bfloat16)
        .reshape(count, kv_count, head_size)
    )
    q_hat, r_q = norm_fwd(q_lin)
    k_hat, r_k = norm_fwd(k_lin)
    index = jnp.arange(count, dtype=jnp.int32)
    place = jnp.where(seg_ids >= 0, index - seg_ids, index).astype(jnp.float32)
    freq = THETA ** (-(jnp.arange(head_size // 2, dtype=jnp.float32) * 2.0) / head_size)
    turn = place[:, None] * freq[None, :]
    turn = jnp.concatenate([turn, turn], -1)[:, None, :]
    cosine = jnp.cos(turn)
    sine = jnp.sin(turn)
    queries = (
        (rotate(q_hat * query_gain, cosine, sine) * scale)
        .astype(jnp.bfloat16)
        .reshape(count, kv_count, group, head_size)
    )
    keys = rotate(k_hat * key_gain, cosine, sine).astype(jnp.bfloat16)
    allowed = (seg_ids[:, None] == seg_ids[None, :]) & (index[None, :] <= index[:, None])

    def scores_of():
        raw = jnp.einsum("qgrd,kgd->grqk", queries, keys, preferred_element_type=jnp.float32)
        return jnp.where(allowed, raw, -1e30)

    scores = scores_of()
    top = jnp.max(scores, -1, keepdims=True)
    expo = jnp.exp(scores - top)
    total = jnp.sum(expo, -1, keepdims=True)
    lse = top + jnp.log(total)
    probs = (expo / total).astype(jnp.bfloat16)
    attended = jnp.einsum("grqk,kgd->qgrd", probs, values, preferred_element_type=jnp.float32)
    attended = attended.reshape(count, q_count * head_size).astype(jnp.bfloat16)
    attended_mine, attended_other = mine(attended), other(attended)
    x_mine = mine(tokens).astype(jnp.float32)
    resid = x_mine + summed(
        jnp.dot(attended_mine, w_out, preferred_element_type=jnp.float32),
        jnp.dot(attended_other, w_out, preferred_element_type=jnp.float32),
    )
    resid_hat, r_resid = norm_fwd(resid)
    inner_mine = (resid_hat * mlp_gain).astype(jnp.bfloat16)
    inner = jnp.concatenate([inner_mine, to_core(inner_mine)], 0)
    gate = jnp.dot(inner, w_gate, preferred_element_type=jnp.float32)
    up = jnp.dot(inner, w_up, preferred_element_type=jnp.float32)
    sig = jax.nn.sigmoid(gate)
    hidden = (gate * sig * up).astype(jnp.bfloat16)
    live = seg_ids >= 0
    grad_mine = jnp.where(mine(live)[:, None], mine(cotangent), 0)
    grad_other = jnp.where(other(live)[:, None], other(cotangent), 0)
    grad_low = jnp.concatenate([grad_mine, grad_other], 0)
    grad_down = scatter(inner_dot(hidden, grad_low).astype(jnp.bfloat16), 1)
    mixed_part = jnp.dot(hidden, w_down, preferred_element_type=jnp.float32)
    mixed = (resid + summed(mixed_part[:half], mixed_part[half:])).astype(jnp.bfloat16)
    mixed = ordered(mixed, to_core(mixed))
    d_hidden = outer_dot(grad_low, w_down)
    d_gate = (d_hidden * up * (sig * (1.0 + gate * (1.0 - sig)))).astype(jnp.bfloat16)
    d_up = (d_hidden * gate * sig).astype(jnp.bfloat16)
    grad_gate = scatter(inner_dot(inner, d_gate).astype(jnp.bfloat16), 0)
    grad_up = scatter(inner_dot(inner, d_up).astype(jnp.bfloat16), 0)
    d_inner = outer_dot(d_gate, w_gate) + outer_dot(d_up, w_up)
    d_inner = summed(d_inner[:half], d_inner[half:])
    grad_mlp_gain = jnp.sum(d_inner * resid_hat, 0)
    d_resid = grad_mine.astype(jnp.float32) + norm_back(d_inner * mlp_gain, resid_hat, r_resid)
    d_branch_mine = d_resid.astype(jnp.bfloat16)
    d_branch = jnp.concatenate([d_branch_mine, to_core(d_branch_mine)], 0)
    attended_mo = jnp.concatenate([attended_mine, attended_other], 0)
    grad_out = scatter(inner_dot(attended_mo, d_branch).astype(jnp.bfloat16), 1)
    d_attended = outer_dot(d_branch, w_out).astype(jnp.bfloat16)
    d_attended = ordered(d_attended[:half], d_attended[half:]).reshape(
        count, kv_count, group, head_size
    )
    kept = jnp.exp(scores_of() - lse)
    kept_low = kept.astype(jnp.bfloat16)
    d_values = jnp.einsum(
        "grqk,qgrd->kgd", kept_low, d_attended, preferred_element_type=jnp.float32
    )
    d_values = d_values.astype(jnp.bfloat16).reshape(count, kv_count * head_size)
    d_probs = jnp.einsum("qgrd,kgd->grqk", d_attended, values, preferred_element_type=jnp.float32)
    d_scores = (kept * (d_probs - jnp.sum(kept * d_probs, -1, keepdims=True))).astype(jnp.bfloat16)
    d_queries = lowered(
        jnp.einsum("grqk,kgd->qgrd", d_scores, keys, preferred_element_type=jnp.float32).reshape(
            count, q_count, head_size
        )
    )
    d_keys = lowered(
        jnp.einsum("grqk,qgrd->kgd", d_scores, queries, preferred_element_type=jnp.float32)
    )
    q_grad = rotate_back(d_queries * scale, cosine, sine)
    k_grad = rotate_back(d_keys, cosine, sine)
    qgain_part = jnp.sum(q_grad * q_hat, (0, 1))
    kgain_part = jnp.sum(k_grad * k_hat, (0, 1))
    d_q_lin = (
        norm_back(q_grad * query_gain, q_hat, r_q)
        .reshape(count, q_count * head_size)
        .astype(jnp.bfloat16)
    )
    d_k_lin = (
        norm_back(k_grad * key_gain, k_hat, r_k)
        .reshape(count, kv_count * head_size)
        .astype(jnp.bfloat16)
    )
    d_lin = jnp.concatenate([d_q_lin, d_k_lin, d_values], 1)
    w_lin = jnp.concatenate([w_query, w_key, w_value], 1)
    grad_lin = scatter(inner_dot(normed, d_lin).astype(jnp.bfloat16), 0)
    q_cols, k_cols = q_count * head_size, kv_count * head_size
    grad_query = grad_lin[:, :q_cols]
    grad_key = grad_lin[:, q_cols : q_cols + k_cols]
    grad_value = grad_lin[:, q_cols + k_cols :]
    d_normed = summed(outer_dot(mine(d_lin), w_lin), outer_dot(other(d_lin), w_lin))
    x_hat_mine, r_x_mine = norm_fwd(x_mine)
    grad_attn_gain = jnp.sum(d_normed * x_hat_mine, 0)
    grad_tokens = (d_resid + norm_back(d_normed * attn_gain, x_hat_mine, r_x_mine)).astype(
        jnp.bfloat16
    )
    grad_tokens = ordered(grad_tokens, to_core(grad_tokens))
    heads = jnp.concatenate([qgain_part, kgain_part])
    heads = heads + to_chip(heads)
    gains = jnp.concatenate([grad_mlp_gain, grad_attn_gain, heads])
    gains = all_sum_dp(n, gains + to_core(gains))
    width = mlp_gain.shape[0]
    my_dp = lax.axis_index("dp")

    def own(begin, size):
        return lax.dynamic_slice(gains, (begin + my_dp * (size // n),), (size // n,))

    return (
        mixed,
        grad_tokens,
        own(width, width),
        grad_query,
        grad_key,
        grad_value,
        grad_out,
        own(0, width),
        grad_gate,
        grad_up,
        grad_down,
        own(2 * width, head_size),
        own(2 * width + head_size, head_size),
    )


def solution(mesh):
    return jax.shard_map(
        functools.partial(on_device, mesh.shape["dp"]),
        mesh=mesh,
        in_specs=(
            P("dp", None),
            P("dp"),
            P("dp", None),
            P(),
            P(None, "tensor"),
            P(None, "tensor"),
            P(None, "tensor"),
            P("tensor", None),
            P(),
            P(None, "tensor"),
            P(None, "tensor"),
            P("tensor", None),
            P(),
            P(),
        ),
        out_specs=(
            P("dp", None),
            P("dp", None),
            P("dp"),
            P("dp", "tensor"),
            P("dp", "tensor"),
            P("dp", "tensor"),
            P("tensor", "dp"),
            P("dp"),
            P("dp", "tensor"),
            P("dp", "tensor"),
            P("tensor", "dp"),
            P("dp"),
            P("dp"),
        ),
        check_vma=False,
    )
```

```python
import functools

import jax
import jax.numpy as jnp
import numpy as np
from jax import lax
from jax.experimental import pallas as pl
from jax.experimental.pallas import tpu as pltpu
from jax.sharding import PartitionSpec as P

EPS = 1e-06
THETA = 1000000.0
CORE_SWAP = ((0, 1), (1, 0), (2, 3), (3, 2))
CHIP_SWAP = ((0, 2), (1, 3), (2, 0), (3, 1))
BLOCK = 256
MIB = 1024 * 1024
COST = pl.CostEstimate(flops=0, bytes_accessed=0, transcendentals=0)


def dot_nn(left, right):
    return jnp.dot(left, right, preferred_element_type=jnp.float32)


def dot_nt(left, right):
    return lax.dot_general(
        left, right, (((1,), (1,)), ((), ())), preferred_element_type=jnp.float32
    )


def dot_tn(left, right):
    return lax.dot_general(
        left, right, (((0,), (0,)), ((), ())), preferred_element_type=jnp.float32
    )


def hbm(value):
    return pltpu.with_memory_space_constraint(value, pltpu.HBM)


def row_mean(value):
    return jnp.mean(value, -1, keepdims=True)


def front_kernel(
    x_ref, gain_ref, wq_ref, wk_ref, wv_ref, cos_ref, sin_ref, qg_ref, kg_ref,
    normed_ref, q_ref, k_ref, v_ref, ql_ref, kl_ref,
):
    size = cos_ref.shape[1]
    x = x_ref[...].astype(jnp.float32)
    factor = lax.rsqrt(row_mean(x * x) + EPS)
    normed = (x * factor * gain_ref[...]).astype(jnp.bfloat16)
    normed_ref[...] = normed
    cosine, sine = cos_ref[...], sin_ref[...]

    def heads(lin, gain, scale, lin_ref, out_ref):
        lin_ref[...] = lin
        for head in range(lin.shape[1] // size):
            cols = slice(head * size, (head + 1) * size)
            part = lin[:, cols]
            scaled = part * lax.rsqrt(row_mean(part * part) + EPS) * gain
            turned = scaled * cosine + pltpu.roll(scaled, size // 2, 1) * sine
            out_ref[:, cols] = (turned * scale).astype(jnp.bfloat16)

    heads(dot_nn(normed, wq_ref[...]), qg_ref[...], size ** (-0.5), ql_ref, q_ref)
    heads(dot_nn(normed, wk_ref[...]), kg_ref[...], 1.0, kl_ref, k_ref)
    v_ref[...] = dot_nn(normed, wv_ref[...]).astype(jnp.bfloat16)


def front(tokens, gain, wq, wk, wv, cosine, sine, q_gain, k_gain):
    count, width = tokens.shape
    size = cosine.shape[1]
    q_cols, k_cols = wq.shape[1], wk.shape[1]

    def rows(cols):
        return pl.BlockSpec((BLOCK, cols), lambda i: (i, 0))

    def whole(*shape):
        return pl.BlockSpec(shape, lambda i: (0,) * len(shape))

    def out(cols, kind):
        return pltpu.HBM((count, cols), kind)

    return pl.pallas_call(
        front_kernel,
        grid=(count // BLOCK,),
        in_specs=[
            rows(width), whole(1, width), whole(width, q_cols), whole(width, k_cols),
            whole(width, k_cols), rows(size), rows(size), whole(1, size), whole(1, size),
        ],
        out_specs=[rows(width), rows(q_cols), rows(k_cols), rows(k_cols), rows(q_cols), rows(k_cols)],
        out_shape=[
            out(width, jnp.bfloat16), out(q_cols, jnp.bfloat16), out(k_cols, jnp.bfloat16),
            out(k_cols, jnp.bfloat16), out(q_cols, jnp.float32), out(k_cols, jnp.float32),
        ],
        compiler_params=pltpu.CompilerParams(vmem_limit_bytes=40 * MIB),
        cost_estimate=COST,
        name="front",
    )(tokens, gain[None, :], wq, wk, wv, cosine, sine, q_gain[None, :], k_gain[None, :])


def pair_rows(value, size):
    return jnp.concatenate([value[:, i : i + size] for i in range(0, value.shape[1], size)], 0)


def placed(number, core_ref):
    spot = number // 2 * 2 + (core_ref[0] ^ (number % 2))
    return pl.ds(pl.multiple_of(spot * BLOCK, BLOCK), BLOCK)


def attend_kernel(first, q_ref, k_ref, v_ref, col_ref, row_ref, out_ref, *prob_refs):
    size = k_ref.shape[1]
    group = q_ref.shape[1] // size
    for number, prob_ref in enumerate(prob_refs):
        begin = (first + number) * BLOCK
        reach = begin + BLOCK
        rows = slice(number * BLOCK, (number + 1) * BLOCK)
        here = lax.broadcasted_iota(jnp.int32, (BLOCK, reach), 0) + begin
        there = lax.broadcasted_iota(jnp.int32, (BLOCK, reach), 1)
        allowed = (col_ref[rows, :] == row_ref[:, :reach]) & (there <= here)
        bias = jnp.where(allowed, 0.0, -1e30)
        queries = q_ref[rows, :]
        for head in range(group):
            cols = slice(head * size, (head + 1) * size)
            expo = jnp.exp(dot_nt(queries[:, cols], k_ref[:reach, :]) + bias)
            share = 1.0 / jnp.sum(expo, -1, keepdims=True)
            probs = (expo * share).astype(jnp.bfloat16)
            prob_ref[0, head * BLOCK : (head + 1) * BLOCK, :] = probs
            out_ref[rows, cols] = dot_nn(probs, v_ref[:reach, :]).astype(jnp.bfloat16)


def attend(queries, keys, values, seg_ids, part, parts):
    count = queries.shape[0]
    size = 128
    heads = keys.shape[1] // size
    group = queries.shape[1] // keys.shape[1]
    rows = count // parts
    blocks = rows // BLOCK
    first = part * blocks
    reach = (part + 1) * rows
    spans = [(first + i + 1) * BLOCK for i in range(blocks)]
    return pl.pallas_call(
        functools.partial(attend_kernel, first),
        grid=(heads,),
        in_specs=[
            pl.BlockSpec((rows, group * size), lambda g: (part, g)),
            pl.BlockSpec((reach, size), lambda g: (0, g)),
            pl.BlockSpec((reach, size), lambda g: (0, g)),
            pl.BlockSpec((rows, 1), lambda g: (part, 0)),
            pl.BlockSpec((1, reach), lambda g: (0, 0)),
        ],
        out_specs=[pl.BlockSpec((rows, group * size), lambda g: (0, g))]
        + [pl.BlockSpec((1, group * BLOCK, span), lambda g: (g, 0, 0)) for span in spans],
        out_shape=[jax.ShapeDtypeStruct((rows, heads * group * size), jnp.bfloat16)]
        + [pltpu.HBM((heads, group * BLOCK, span), jnp.bfloat16) for span in spans],
        compiler_params=pltpu.CompilerParams(vmem_limit_bytes=40 * MIB),
        cost_estimate=COST,
        name="attend",
    )(hbm(queries), hbm(keys), hbm(values), seg_ids[:, None], seg_ids[None, :])


def attend_back_kernel(blocks, *refs):
    core_ref, g_ref, q_ref, k_ref, v_ref, ql_ref, kl_ref, cos_ref, sin_ref, qg_ref, kg_ref = refs[:11]
    prob_refs = refs[11 : 11 + blocks]
    dq_out, dk_out, dv_out, gains_ref, dk_ref, dv_ref = refs[-6:]
    size = k_ref.shape[1]
    group = q_ref.shape[1] // size

    def turned_back(value, rows):
        value = value.astype(jnp.bfloat16).astype(jnp.float32)
        return value * cos_ref[rows, :] - pltpu.roll(value, size // 2, 1) * sin_ref[rows, :]

    def unnorm(grad, lin, gain):
        factor = lax.rsqrt(row_mean(lin * lin) + EPS)
        hat = lin * factor
        scaled = grad * gain
        back = factor * (scaled - hat * row_mean(scaled * hat))
        return back.astype(jnp.bfloat16), jnp.sum(grad * hat, 0, keepdims=True)

    dk_ref[...] = jnp.zeros_like(dk_ref)
    dv_ref[...] = jnp.zeros_like(dv_ref)
    q_sum = jnp.zeros((1, size), jnp.float32)
    for number in range(blocks):
        rows = slice(number * BLOCK, (number + 1) * BLOCK)
        reach = (number + 1) * BLOCK
        for head in range(group):
            cols = slice(head * size, (head + 1) * size)
            grad = g_ref[placed(number, core_ref), cols]
            probs = prob_refs[number][0, head * BLOCK : (head + 1) * BLOCK, :]
            d_probs = dot_nt(grad, v_ref[:reach, :])
            probs_wide = probs.astype(jnp.float32)
            both = probs_wide * d_probs
            d_scores = (both - probs_wide * jnp.sum(both, -1, keepdims=True)).astype(jnp.bfloat16)
            dv_ref[:reach, :] += dot_tn(probs, grad)
            dk_ref[:reach, :] += dot_tn(d_scores, q_ref[rows, cols])
            d_query = dot_nn(d_scores, k_ref[:reach, :])
            turned = turned_back(d_query, rows)
            back, total = unnorm(turned * size ** (-0.5), ql_ref[rows, cols], qg_ref[...])
            dq_out[rows, cols] = back
            q_sum = q_sum + total
    turned = turned_back(dk_ref[...], slice(None))
    back, k_sum = unnorm(turned, kl_ref[...], kg_ref[...])
    dk_out[...] = back
    dv_out[...] = dv_ref[...].astype(jnp.bfloat16)
    gains_ref[0:1, :] = q_sum
    gains_ref[1:2, :] = k_sum
    gains_ref[2:, :] = jnp.zeros((6, size), jnp.float32)


def attend_back(core, grad, queries, keys, values, q_lin, k_lin, cosine, sine, q_gain, k_gain, probs, g, before):
    count = queries.shape[0]
    size = cosine.shape[1]
    group = queries.shape[1] // keys.shape[1]
    blocks = len(probs)

    def cols(width):
        return pl.BlockSpec((count, width), lambda i: (0, g))

    def whole(rows):
        return pl.BlockSpec((rows, size), lambda i: (0, 0))

    return pl.pallas_call(
        functools.partial(attend_back_kernel, blocks),
        grid=(1,),
        in_specs=[
            pl.BlockSpec(memory_space=pltpu.SMEM),
            cols(group * size), cols(group * size), cols(size), cols(size), cols(group * size),
            cols(size), whole(count), whole(count), whole(1), whole(1),
        ]
        + [pl.BlockSpec((1, *p.shape[1:]), lambda i: (g, 0, 0)) for p in probs]
        + [pl.BlockSpec(memory_space=pl.ANY)] * len(before),
        out_specs=[cols(group * size), cols(size), cols(size), whole(8)],
        out_shape=[
            jax.ShapeDtypeStruct(queries.shape, jnp.bfloat16),
            jax.ShapeDtypeStruct(keys.shape, jnp.bfloat16),
            jax.ShapeDtypeStruct(keys.shape, jnp.bfloat16),
            jax.ShapeDtypeStruct((8, size), jnp.float32),
        ],
        input_output_aliases={11 + blocks + i: i for i in range(len(before))},
        scratch_shapes=[pltpu.VMEM((count, size), jnp.float32)] * 2,
        compiler_params=pltpu.CompilerParams(vmem_limit_bytes=40 * MIB),
        cost_estimate=COST,
        name="attend_back",
    )(
        core, grad, hbm(queries), hbm(keys), hbm(values), hbm(q_lin), hbm(k_lin), cosine, sine,
        q_gain[None, :], k_gain[None, :], *[hbm(p) for p in probs], *before,
    )


def feed_kernel(mine_ref, other_ref, wg_ref, wu_ref, dh_ref, *refs):
    inner_ref, hidden_ref, dg_ref, du_ref = refs[-4:]
    inner = jnp.concatenate([mine_ref[...], other_ref[...]], 0)

    @pl.when(pl.program_id(0) == 0)
    def _():
        inner_ref[...] = inner

    gate = dot_nn(inner, wg_ref[...])
    up = dot_nn(inner, wu_ref[...])
    sig = 1.0 / (1.0 + jnp.exp(-gate))
    silu = gate * sig
    d_hidden = dh_ref[...].astype(jnp.float32)
    hidden_ref[...] = (silu * up).astype(jnp.bfloat16)
    du_ref[...] = (d_hidden * silu).astype(jnp.bfloat16)
    dg_ref[...] = (d_hidden * up * (sig + silu * (1.0 - sig))).astype(jnp.bfloat16)


def feed(mine, other, w_gate, w_up, d_hidden, part, before, cols=512):
    rows, width = mine.shape
    count, units = d_hidden.shape
    here = pl.BlockSpec((2 * rows, width), lambda j: (part, 0))
    block = pl.BlockSpec((2 * rows, cols), lambda j: (part, j))
    weight = pl.BlockSpec((width, cols), lambda j: (0, j))
    half = pl.BlockSpec((rows, width), lambda j: (0, 0))
    out = jax.ShapeDtypeStruct((count, units), jnp.bfloat16)
    return pl.pallas_call(
        feed_kernel,
        grid=(units // cols,),
        in_specs=[half, half, weight, weight, block]
        + [pl.BlockSpec(memory_space=pl.ANY)] * len(before),
        out_specs=[here, block, block, block],
        out_shape=[jax.ShapeDtypeStruct((count, width), jnp.bfloat16), out, out, out],
        input_output_aliases={5 + i: i for i in range(len(before))},
        compiler_params=pltpu.CompilerParams(vmem_limit_bytes=40 * MIB),
        cost_estimate=COST,
        name="feed",
    )(mine, other, w_gate, w_up, d_hidden, *before)


ROWS = 128


def rows_call(kernel, name, rows, ins, outs):
    def spec(shape):
        if shape[0] == rows:
            return pl.BlockSpec((ROWS, shape[1]), lambda i: (i, 0))
        return pl.BlockSpec(shape, lambda i: (0, 0))

    return pl.pallas_call(
        kernel,
        grid=(rows // ROWS,),
        in_specs=[spec(a.shape) for a in ins],
        out_specs=[spec(o.shape) for o in outs],
        out_shape=outs,
        compiler_params=pltpu.CompilerParams(vmem_limit_bytes=24 * MIB),
        cost_estimate=COST,
        name=name,
    )(*ins)


def wide(ref):
    return ref[...].astype(jnp.float32)


def settle_kernel(x_ref, near_ref, far_ref, gain_ref, resid_ref, inner_ref):
    resid = wide(x_ref) + (wide(near_ref) + wide(far_ref))
    resid_ref[...] = resid
    factor = lax.rsqrt(row_mean(resid * resid) + EPS)
    inner_ref[...] = (resid * factor * gain_ref[...]).astype(jnp.bfloat16)


def settle(x, near, far, gain):
    rows, width = x.shape
    return rows_call(
        settle_kernel, "settle", rows, (x, near, far, gain[None, :]),
        [jax.ShapeDtypeStruct((rows, width), jnp.float32), jax.ShapeDtypeStruct((rows, width), jnp.bfloat16)],
    )


def unsettle_kernel(near_ref, far_ref, resid_ref, grad_ref, gain_ref, out_ref, low_ref, sum_ref):
    @pl.when(pl.program_id(0) == 0)
    def _():
        sum_ref[...] = jnp.zeros_like(sum_ref)

    resid = resid_ref[...].astype(jnp.float32)
    factor = lax.rsqrt(row_mean(resid * resid) + EPS)
    hat = resid * factor
    d_inner = wide(near_ref) + wide(far_ref)
    both = d_inner * hat
    sum_ref[0:1, :] += jnp.sum(both, 0, keepdims=True)
    scaled = d_inner * gain_ref[...]
    back = wide(grad_ref) + factor * (scaled - hat * row_mean(both * gain_ref[...]))
    out_ref[...] = back.astype(out_ref.dtype)
    if low_ref is not None:
        low_ref[...] = back.astype(jnp.bfloat16)


def last_kernel(near_ref, far_ref, resid_ref, grad_ref, gain_ref, out_ref, sum_ref):
    unsettle_kernel(near_ref, far_ref, resid_ref, grad_ref, gain_ref, out_ref, None, sum_ref)


def unsettle(near, far, resid, grad, gain):
    rows, width = near.shape
    return rows_call(
        unsettle_kernel, "unsettle", rows, (near, far, resid, grad, gain[None, :]),
        [
            jax.ShapeDtypeStruct((rows, width), jnp.float32),
            jax.ShapeDtypeStruct((rows, width), jnp.bfloat16),
            jax.ShapeDtypeStruct((8, width), jnp.float32),
        ],
    )


def unsettle_last(near, far, resid, grad, gain):
    rows, width = near.shape
    return rows_call(
        last_kernel, "unsettle_last", rows, (near, far, resid, grad, gain[None, :]),
        [jax.ShapeDtypeStruct((rows, width), jnp.bfloat16), jax.ShapeDtypeStruct((8, width), jnp.float32)],
    )


def live_rows_kernel(core_ref, value_ref, seg_ref, out_ref):
    out_ref[...] = jnp.where(seg_ref[...] >= 0, value_ref[...].astype(jnp.float32), 0.0).astype(jnp.bfloat16)


def live_rows(core, value, seg_ids):
    count, width = value.shape

    def from_block(i, core_ref):
        return (i ^ core_ref[0], 0)

    return pl.pallas_call(
        live_rows_kernel,
        grid_spec=pltpu.PrefetchScalarGridSpec(
            num_scalar_prefetch=1,
            grid=(count // BLOCK,),
            in_specs=[pl.BlockSpec((BLOCK, width), from_block), pl.BlockSpec((BLOCK, 1), from_block)],
            out_specs=pl.BlockSpec((BLOCK, width), lambda i, core_ref: (i, 0)),
        ),
        out_shape=jax.ShapeDtypeStruct((count, width), jnp.bfloat16),
        compiler_params=pltpu.CompilerParams(vmem_limit_bytes=24 * MIB),
        cost_estimate=COST,
        name="live_rows",
    )(core, value, seg_ids[:, None])


def ring_of(n):
    order = list(range(0, n, 2)) + [i for i in range(n - 1, 0, -1) if i % 2]
    place = [0] * n
    for spot, index in enumerate(order):
        place[index] = spot
    ahead = tuple((order[i], order[(i + 1) % n]) for i in range(n))
    back = tuple((b, a) for a, b in ahead)
    return order, place, ahead, back


def ring_table(n):
    order, place, _, _ = ring_of(n)
    table = [
        [[order[(place[i] - 1 - s) % n], order[(place[i] + 1 + s) % n]] for s in range(n)]
        for i in range(n)
    ]
    return jnp.asarray(np.array(table, np.int32).reshape(n, 2 * n))[lax.axis_index("dp")]


def ring_kernel(finish, step, *refs):
    where_ref, part_ref = refs[0], refs[-4]
    own_a, own_b, sem = refs[-3:]
    size, half = own_a.shape
    copies = []
    for side, own in enumerate((own_a, own_b)):
        begin = pl.multiple_of(where_ref[2 * step + side] * size, size)
        piece = part_ref.at[pl.ds(begin, size), pl.ds(side * half, half)]
        copies.append(pltpu.make_async_copy(piece, own, sem.at[side]))
    for copy in copies:
        copy.start()
    for copy in copies:
        copy.wait()
    finish(own_a, own_b, *refs[1:-4])


def ring_first(own_a, own_b, out_a_ref, out_b_ref):
    out_a_ref[...] = own_a[...]
    out_b_ref[...] = own_b[...]


def ring_add(own_a, own_b, came_a_ref, came_b_ref, out_a_ref, out_b_ref):
    out_a_ref[...] = (wide(came_a_ref) + wide(own_a)).astype(jnp.bfloat16)
    out_b_ref[...] = (wide(came_b_ref) + wide(own_b)).astype(jnp.bfloat16)


def ring_last(own_a, own_b, came_a_ref, came_b_ref, out_ref):
    half = own_a.shape[1]
    out_ref[:, :half] = wide(came_a_ref) + wide(own_a)
    out_ref[:, half:] = wide(came_b_ref) + wide(own_b)


def ring_last_turned(own_a, own_b, came_a_ref, came_b_ref, out_ref):
    half = own_a.shape[1]
    out_ref[:half, :] = (wide(came_a_ref) + wide(own_a)).T
    out_ref[half:, :] = (wide(came_b_ref) + wide(own_b)).T


def ring_last_lin(own_a, own_b, came_a_ref, came_b_ref, out_ref, q_ref, k_ref, v_ref):
    whole = jnp.concatenate([wide(came_a_ref) + wide(own_a), wide(came_b_ref) + wide(own_b)], 1)
    begin = 0
    for ref in (out_ref, q_ref, k_ref, v_ref):
        width = ref.shape[0] if ref is out_ref else ref.shape[1]
        part = whole[:, begin : begin + width]
        ref[...] = part.T if ref is out_ref else part
        begin += width


def ring_call(finish, n, where, step, came, part, out_shape):
    size, half = part.shape[0] // n, part.shape[1] // 2

    def kernel(*refs):
        outs = len(jax.tree.leaves(out_shape))
        ins = 1 + len(came)
        ring_kernel(
            finish, step, *refs[:ins], *refs[ins + 1 : ins + 1 + outs], refs[ins], *refs[ins + 1 + outs :]
        )

    return pl.pallas_call(
        kernel,
        in_specs=[pl.BlockSpec(memory_space=pltpu.SMEM)]
        + [pl.BlockSpec(memory_space=pltpu.VMEM)] * len(came)
        + [pl.BlockSpec(memory_space=pltpu.HBM)],
        out_specs=jax.tree.map(lambda o: pl.BlockSpec(memory_space=pltpu.VMEM), out_shape),
        out_shape=out_shape,
        scratch_shapes=[
            pltpu.VMEM((size, half), jnp.bfloat16),
            pltpu.VMEM((size, half), jnp.bfloat16),
            pltpu.SemaphoreType.DMA((2,)),
        ],
        compiler_params=pltpu.CompilerParams(vmem_limit_bytes=16 * MIB),
        cost_estimate=COST,
        name=finish.__name__,
    )(where, *came, hbm(part))


class Order:
    def __init__(self):
        self.last = None

    def run(self, piece, first, *rest):
        if self.last is not None:
            first, _ = lax.optimization_barrier((first, self.last))
        out = piece(first, *rest)
        self.last = jax.tree.leaves(out)[0]
        return out


    def tie(self, value):
        return lax.optimization_barrier((value, self.last))[0]


class Ring:
    def __init__(self, n, where, order, part, last, last_shapes):
        self.n, self.where, self.order, self.part = n, where, order, part
        self.last, self.last_shapes = last, last_shapes
        self.step_no = 0
        _, _, self.ahead, self.back = ring_of(n)
        size, half = part.shape[0] // n, part.shape[1] // 2
        self.out = [jax.ShapeDtypeStruct((size, half), jnp.bfloat16)] * 2
        self.send(self.call(ring_first, self.out))

    def call(self, finish, out):
        if self.step_no == 0:
            return self.order.run(
                lambda p: ring_call(finish, self.n, self.where, 0, (), p, out), self.part
            )
        return self.order.run(
            lambda a: ring_call(
                finish, self.n, self.where, self.step_no, (a, self.came[1]), self.part, out
            ),
            self.came[0],
        )

    def send(self, held):
        self.came = (lax.ppermute(held[0], "dp", self.ahead), lax.ppermute(held[1], "dp", self.back))

    def step(self):
        if self.step_no < self.n - 1:
            self.step_no += 1
            if self.step_no < self.n - 1:
                self.send(self.call(ring_add, self.out))
            else:
                self.result = self.call(self.last, self.last_shapes)

    def finish(self):
        while self.step_no < self.n - 1:
            self.step()
        return self.result


DOTS = {"nn": dot_nn, "nt": dot_nt, "tn": dot_tn}


def pairs_kernel(kind, outs, count, core_ref, *refs):
    out_refs = refs[-len(outs) :]
    for (spots, _), out_ref in zip(outs, out_refs):
        for i, spot in enumerate(spots):
            if spot < 0:
                rows = pl.ds(pl.multiple_of(((-1 - spot) ^ core_ref[0]) * BLOCK, BLOCK), BLOCK)
            else:
                rows = slice(spot * BLOCK, (spot + 1) * BLOCK)
            total = None
            for left_ref, right_ref in zip(refs[: 2 * count : 2], refs[1 : 2 * count : 2]):
                value = DOTS[kind](left_ref[rows, :], right_ref[...])
                total = value if total is None else total + value
            out_ref[i * BLOCK : (i + 1) * BLOCK, :] = total.astype(out_ref.dtype)


def pairs(core, kind, terms, outs, part=0, parts=1, before=(), cols=512):
    width = terms[0][1].shape[1 if kind == "nn" else 0]
    steps = width // cols // parts
    begin = part * steps
    ins, specs = [], []
    for left, right in terms:
        ins += [left, right]
        specs.append(pl.BlockSpec(left.shape, lambda j: (0, 0)))
        if kind == "nn":
            specs.append(pl.BlockSpec((right.shape[0], cols), lambda j: (0, begin + j)))
        else:
            specs.append(pl.BlockSpec((cols, right.shape[1]), lambda j: (begin + j, 0)))
    return pl.pallas_call(
        functools.partial(pairs_kernel, kind, outs, len(terms)),
        grid=(steps,),
        in_specs=[pl.BlockSpec(memory_space=pltpu.SMEM)]
        + specs
        + [pl.BlockSpec(memory_space=pl.ANY)] * len(before),
        out_specs=[pl.BlockSpec((len(o[0]) * BLOCK, cols), lambda j: (0, begin + j)) for o in outs],
        out_shape=[jax.ShapeDtypeStruct((len(o[0]) * BLOCK, width), o[1]) for o in outs],
        input_output_aliases={1 + len(ins) + i: i for i in range(len(before))},
        compiler_params=pltpu.CompilerParams(vmem_limit_bytes=40 * MIB),
        cost_estimate=COST,
        name="pairs",
    )(core, *[hbm(i) for i in ins], *before)


def near_kernel(mine_ref, came_ref, out_ref):
    out_ref[...] = (mine_ref[...] + wide(came_ref)).astype(jnp.bfloat16)


def near_add(came, mine):
    return rows_call(
        near_kernel, "near_add", mine.shape[0], (mine, came),
        [jax.ShapeDtypeStruct(mine.shape, jnp.bfloat16)],
    )[0]


def mixed_kernel(resid_ref, near_ref, far_ref, out_ref):
    out_ref[...] = (resid_ref[...] + (wide(near_ref) + wide(far_ref))).astype(jnp.bfloat16)


def nt_kernel(*refs):
    out_ref = refs[-1]
    begin = 0
    for left_ref in refs[1:-1]:
        rows = slice(begin, begin + left_ref.shape[0])
        out_ref[rows, :] = dot_nt(left_ref[...], refs[0][...]).astype(jnp.bfloat16)
        begin += left_ref.shape[0]


def times_turned(lefts, right, cols=512):
    rows = sum(left.shape[0] for left in lefts)
    return pl.pallas_call(
        nt_kernel,
        grid=(right.shape[0] // cols,),
        in_specs=[pl.BlockSpec((cols, right.shape[1]), lambda j: (j, 0))]
        + [pl.BlockSpec(left.shape, lambda j: (0, 0)) for left in lefts],
        out_specs=pl.BlockSpec((rows, cols), lambda j: (0, j)),
        out_shape=jax.ShapeDtypeStruct((rows, right.shape[0]), jnp.bfloat16),
        compiler_params=pltpu.CompilerParams(vmem_limit_bytes=40 * MIB),
        cost_estimate=COST,
        name="times_turned",
    )(right, *lefts)


def weight_grad_kernel(counts, *refs):
    out_ref = refs[-1]
    at, begin = 0, 0
    for lefts, rights in counts:
        left = refs[at][...]
        if lefts > 1:
            left = jnp.concatenate([ref[...] for ref in refs[at : at + lefts]], 0)
        for ref in refs[at + lefts : at + lefts + rights]:
            width = ref.shape[1]
            out_ref[:, begin : begin + width] = dot_tn(left, ref[...]).astype(jnp.bfloat16)
            begin += width
        at += lefts + rights


def weight_grad(groups, rows=256):
    width = groups[0][0][0].shape[1]
    ins, specs, cols = [], [], 0
    for lefts, rights in groups:
        ins += [*lefts, *rights]
        specs += [pl.BlockSpec((left.shape[0], rows), lambda i: (0, i)) for left in lefts]
        specs += [pl.BlockSpec(right.shape, lambda i: (0, 0)) for right in rights]
        cols += sum(right.shape[1] for right in rights)
    return pl.pallas_call(
        functools.partial(weight_grad_kernel, [(len(a), len(b)) for a, b in groups]),
        grid=(width // rows,),
        in_specs=specs,
        out_specs=pl.BlockSpec((rows, cols), lambda i: (i, 0)),
        out_shape=jax.ShapeDtypeStruct((width, cols), jnp.bfloat16),
        compiler_params=pltpu.CompilerParams(vmem_limit_bytes=32 * MIB),
        cost_estimate=COST,
        name="weight_grad",
    )(*[hbm(i) for i in ins])


def join_kernel(core_ref, mine_ref, other_ref, out_ref):
    @pl.when(pl.program_id(0) % 2 == 0)
    def _():
        out_ref[...] = mine_ref[...]

    @pl.when(pl.program_id(0) % 2 == 1)
    def _():
        out_ref[...] = other_ref[...]


def join(other, core, mine):
    rows, width = mine.shape
    block = pl.BlockSpec((BLOCK, width), lambda i, core_ref: (i >> 1, 0))
    return pl.pallas_call(
        join_kernel,
        grid_spec=pltpu.PrefetchScalarGridSpec(
            num_scalar_prefetch=1,
            grid=(2 * rows // BLOCK,),
            in_specs=[block, block],
            out_specs=pl.BlockSpec((BLOCK, width), lambda i, core_ref: (i ^ core_ref[0], 0)),
        ),
        out_shape=jax.ShapeDtypeStruct((2 * rows, width), mine.dtype),
        compiler_params=pltpu.CompilerParams(vmem_limit_bytes=24 * MIB),
        cost_estimate=COST,
        name="join",
    )(core, mine, other)


def to_core(value, pieces=1):
    share = value.shape[0] // pieces
    cut = [value[i * share : (i + 1) * share] for i in range(pieces)]
    came = [lax.ppermute(c, "tensor", CORE_SWAP) for c in cut]
    return jnp.concatenate(came, 0) if pieces > 1 else came[0]


def to_chip(value):
    return lax.ppermute(value, "tensor", CHIP_SWAP)


def low(value):
    return value.astype(jnp.bfloat16)


def all_sum_dp(n, value):
    step = 1
    while step < n:
        value = value + lax.ppermute(value, "dp", tuple((i, i ^ step) for i in range(n)))
        step *= 2
    return value


def on_device(
    n, tokens, seg_ids, cotangent, attn_gain, w_query, w_key, w_value, w_out, mlp_gain, w_gate, w_up,
    w_down, query_gain, key_gain,
):
    count, width = tokens.shape
    size = query_gain.shape[0]
    parts = 2
    rows = count // parts
    core_no = lax.axis_index("tensor") % 2
    core = core_no.astype(jnp.int32)[None]
    where = ring_table(n)
    order = Order()
    run = order.run

    def both_parts(piece):
        return [piece(j) for j in range(parts)]

    def own_rows(value, part, other=0):
        begin = part * rows + (core_no ^ other) * BLOCK
        return lax.dynamic_slice_in_dim(value, begin, BLOCK, 0)

    index = jnp.arange(count, dtype=jnp.int32)
    place = jnp.where(seg_ids >= 0, index - seg_ids, index).astype(jnp.float32)
    freq = THETA ** (-(jnp.arange(size // 2, dtype=jnp.float32) * 2.0) / size)
    turn = place[:, None] * freq[None, :]
    cosine, sine = jnp.cos(turn), jnp.sin(turn)
    cosine, sine = jnp.concatenate([cosine, cosine], -1), jnp.concatenate([-sine, sine], -1)

    normed, queries, keys, values, q_lin, k_lin = run(
        front, tokens, attn_gain, w_query, w_key, w_value, cosine, sine, query_gain, key_gain
    )
    wide_low = (jnp.float32, jnp.bfloat16)

    def mine_other(mine, other):
        return ((mine, wide_low[0]), (other, wide_low[1]))

    attended, probs, near, far = [], [], [], []
    for j in range(parts):
        out = run(lambda q: attend(q, keys, values, seg_ids, j, parts), queries)
        attended.append(out[0])
        probs += out[1:]
        mine, other = run(lambda a: pairs(core, "nn", [(a, w_out)], mine_other((-1,), (-2,))), out[0])
        near.append(run(near_add, to_core(other, 4), mine))
        far.append(to_chip(near[j]))

    grad_low = run(lambda c: live_rows(core, c, seg_ids), cotangent)
    d_hidden = run(lambda g: times_turned([g], w_down), grad_low)
    x_own = both_parts(lambda j: own_rows(tokens, j))

    resid, fed = [], ()
    for j in range(parts):
        held, inner_own = run(lambda f: settle(x_own[j], near[j], f, mlp_gain), far[j])
        resid.append(held)
        inner_other = to_core(inner_own, 4)
        fed = run(lambda o: feed(inner_own, o, w_gate, w_up, d_hidden, j, fed), inner_other)
    inner, hidden, d_gate, d_up = fed

    def shape(*extent):
        return jax.ShapeDtypeStruct(extent, jnp.float32)

    units, share = w_gate.shape[1], width // n
    q_cols, k_cols = w_query.shape[1], w_key.shape[1]
    active, results = [], {}

    def ring(name, part, last, last_shapes):
        active.append((name, Ring(n, where, order, part, last, last_shapes)))

    def tick():
        for item in list(active):
            item[1].step()
            if item[1].step_no == n - 1:
                results[item[0]] = item[1].result
                active.remove(item)

    down_part = run(lambda h: weight_grad([([grad_low], [h])]), hidden)
    ring("down", down_part, ring_last_turned, shape(units, share))
    made = ()
    for half in range(2):
        made = run(
            lambda d: pairs(
                core, "nt", [(d, w_gate), (d_up, w_up)], mine_other((0, 2), (1, 3)), half, 2, made
            ),
            d_gate,
        )
        tick()
    came3 = to_core(order.tie(made[1]))
    gate_part = run(lambda d: weight_grad([([inner], [d])]), d_gate)
    tick()
    near3 = run(near_add, came3, made[0])
    far3 = to_chip(near3)
    ring("gate", gate_part, ring_last, shape(share, units))
    up_part = run(lambda d: weight_grad([([inner], [d])]), d_up)
    tick()
    mixed_mine, mixed_other = run(
        lambda h: pairs(core, "nn", [(h, w_down)], mine_other((0, 2), (1, 3))), hidden
    )
    tick()
    blocks = [part[i : i + BLOCK] for part in attended for i in range(0, rows, BLOCK)]
    attended_mine_first = jnp.where(
        core_no == 0,
        jnp.concatenate(blocks, 0),
        jnp.concatenate([blocks[i ^ 1] for i in range(len(blocks))], 0),
    )
    grad_own = jnp.concatenate([grad_low[j * rows : j * rows + BLOCK] for j in range(parts)], 0)
    resid_own = jnp.concatenate(resid, 0)
    tick()
    d_resid, branch_own, mlp_sums = run(
        lambda f: unsettle(near3, f, resid_own, grad_own, mlp_gain), far3
    )
    both = to_core(jnp.concatenate([branch_own, order.tie(mixed_other)], 0))
    branch_other, came2 = both[: branch_own.shape[0]], both[branch_own.shape[0] :]
    tick()
    ring("up", up_part, ring_last, shape(share, units))
    near2 = run(near_add, came2, mixed_mine)
    far2 = to_chip(near2)
    d_branch = [b[j * BLOCK : (j + 1) * BLOCK] for j in range(parts) for b in (branch_own, branch_other)]
    d_attended = run(lambda d: times_turned([*d_branch[:-1], d], w_out), d_branch[-1])
    heads_count = k_cols // size
    d_lin, gain_sums = (), jnp.zeros((8, size), jnp.float32)
    for g in range(heads_count):
        *d_lin, total = run(
            lambda a: attend_back(
                core, a, queries, keys, values, q_lin, k_lin, cosine, sine, query_gain, key_gain,
                probs, g, d_lin,
            ),
            d_attended,
        )
        gain_sums = gain_sums + total
        tick()
    d_q_lin, d_k_lin, d_values = d_lin
    lin_part = run(
        lambda d: weight_grad([(d_branch, [attended_mine_first]), ([normed], [d, d_k_lin, d_values])]),
        d_q_lin,
    )
    mine, other = run(
        lambda d: pairs(
            core, "nt", [(d, w_query), (d_k_lin, w_key), (d_values, w_value)],
            mine_other((-1, -3), (-2, -4)),
        ),
        d_q_lin,
    )
    tick()
    ring(
        "lin", lin_part, ring_last_lin,
        [shape(q_cols, share), shape(share, q_cols), shape(share, k_cols), shape(share, k_cols)],
    )
    mixed = run(lambda f, n_, r: rows_call(
        mixed_kernel, "mixed", n_.shape[0], (r, n_, f), [jax.ShapeDtypeStruct(n_.shape, jnp.bfloat16)]
    )[0], far2, near2, resid_own)
    both = to_core(jnp.concatenate([mixed, order.tie(other)], 0))
    mixed_far, came4 = both[: mixed.shape[0]], both[mixed.shape[0] :]
    tick()
    near4 = run(near_add, came4, mine)
    far4 = to_chip(near4)
    mixed = run(join, mixed_far, core, mixed)
    tick()
    tick()
    tick()
    grad_tokens, attn_sums = run(
        lambda f: unsettle_last(near4, f, jnp.concatenate(x_own, 0), d_resid, attn_gain), far4
    )
    grad_tokens_other = to_core(grad_tokens)
    heads_sum = gain_sums[:2].reshape(-1)
    heads_sum = heads_sum + to_chip(heads_sum)
    gains = jnp.concatenate([mlp_sums[0], attn_sums[0], heads_sum])
    tick()
    grad_tokens = run(join, grad_tokens_other, core, grad_tokens)
    gains = all_sum_dp(n, gains + to_core(gains))
    while active:
        tick()
    my_dp = lax.axis_index("dp")

    def own(begin, extent):
        return lax.dynamic_slice(gains, (begin + my_dp * (extent // n),), (extent // n,))

    grad_out, grad_query, grad_key, grad_value = results["lin"]
    return (
        mixed,
        grad_tokens,
        own(width, width),
        grad_query,
        grad_key,
        grad_value,
        grad_out,
        own(0, width),
        results["gate"],
        results["up"],
        results["down"],
        own(2 * width, size),
        own(2 * width + size, size),
    )


def solution(mesh):
    rows, cols = P("dp", "tensor"), P("tensor", "dp")
    return jax.shard_map(
        functools.partial(on_device, mesh.shape["dp"]),
        mesh=mesh,
        in_specs=(
            P("dp", None), P("dp"), P("dp", None), P(), P(None, "tensor"), P(None, "tensor"),
            P(None, "tensor"), P("tensor", None), P(), P(None, "tensor"), P(None, "tensor"),
            P("tensor", None), P(), P(),
        ),
        out_specs=(
            P("dp", None), P("dp", None), P("dp"), rows, rows, rows, cols, P("dp"), rows, rows, cols,
            P("dp"), P("dp"),
        ),
        check_vma=False,
    )
```

```python
import functools

import jax
import jax.numpy as jnp
import numpy as np
from jax import lax
from jax.experimental import pallas as pl
from jax.experimental.pallas import tpu as pltpu
from jax.sharding import PartitionSpec as P

EPS = 1e-06
THETA = 1000000.0
CORE_SWAP = ((0, 1), (1, 0), (2, 3), (3, 2))
CHIP_SWAP = ((0, 2), (1, 3), (2, 0), (3, 1))
BLOCK = 256
MIB = 1024 * 1024
COST = pl.CostEstimate(flops=0, bytes_accessed=0, transcendentals=0)


def dot_nn(left, right):
    return jnp.dot(left, right, preferred_element_type=jnp.float32)


def dot_nt(left, right):
    return lax.dot_general(
        left, right, (((1,), (1,)), ((), ())), preferred_element_type=jnp.float32
    )


def dot_tn(left, right):
    return lax.dot_general(
        left, right, (((0,), (0,)), ((), ())), preferred_element_type=jnp.float32
    )


def hbm(value):
    return pltpu.with_memory_space_constraint(value, pltpu.HBM)


def row_mean(value):
    return jnp.mean(value, -1, keepdims=True)


def front_kernel(
    x_ref, gain_ref, wq_ref, wk_ref, wv_ref, cos_ref, sin_ref, qg_ref, kg_ref,
    normed_ref, q_ref, k_ref, v_ref, ql_ref, kl_ref,
):
    size = cos_ref.shape[1]
    x = x_ref[...].astype(jnp.float32)
    factor = lax.rsqrt(row_mean(x * x) + EPS)
    normed = (x * factor * gain_ref[...]).astype(jnp.bfloat16)
    normed_ref[...] = normed
    cosine, sine = cos_ref[...], sin_ref[...]

    def heads(lin, gain, scale, lin_ref, out_ref):
        lin_ref[...] = lin
        for head in range(lin.shape[1] // size):
            cols = slice(head * size, (head + 1) * size)
            part = lin[:, cols]
            scaled = part * lax.rsqrt(row_mean(part * part) + EPS) * gain
            turned = scaled * cosine + pltpu.roll(scaled, size // 2, 1) * sine
            out_ref[:, cols] = (turned * scale).astype(jnp.bfloat16)

    heads(dot_nn(normed, wq_ref[...]), qg_ref[...], size ** (-0.5), ql_ref, q_ref)
    heads(dot_nn(normed, wk_ref[...]), kg_ref[...], 1.0, kl_ref, k_ref)
    v_ref[...] = dot_nn(normed, wv_ref[...]).astype(jnp.bfloat16)


def front(tokens, gain, wq, wk, wv, cosine, sine, q_gain, k_gain):
    count, width = tokens.shape
    size = cosine.shape[1]
    q_cols, k_cols = wq.shape[1], wk.shape[1]

    def rows(cols):
        return pl.BlockSpec((BLOCK, cols), lambda i: (i, 0))

    def whole(*shape):
        return pl.BlockSpec(shape, lambda i: (0,) * len(shape))

    def out(cols, kind):
        return pltpu.HBM((count, cols), kind)

    return pl.pallas_call(
        front_kernel,
        grid=(count // BLOCK,),
        in_specs=[
            rows(width), whole(1, width), whole(width, q_cols), whole(width, k_cols),
            whole(width, k_cols), rows(size), rows(size), whole(1, size), whole(1, size),
        ],
        out_specs=[rows(width), rows(q_cols), rows(k_cols), rows(k_cols), rows(q_cols), rows(k_cols)],
        out_shape=[
            out(width, jnp.bfloat16), out(q_cols, jnp.bfloat16), out(k_cols, jnp.bfloat16),
            out(k_cols, jnp.bfloat16), out(q_cols, jnp.float32), out(k_cols, jnp.float32),
        ],
        compiler_params=pltpu.CompilerParams(vmem_limit_bytes=40 * MIB),
        cost_estimate=COST,
        name="front",
    )(
        hbm(tokens), gain[None, :], hbm(wq), hbm(wk), hbm(wv), cosine, sine, q_gain[None, :],
        k_gain[None, :],
    )


def pair_rows(value, size):
    return jnp.concatenate([value[:, i : i + size] for i in range(0, value.shape[1], size)], 0)


def placed(number, core_ref):
    spot = number // 2 * 2 + (core_ref[0] ^ (number % 2))
    return pl.ds(pl.multiple_of(spot * BLOCK, BLOCK), BLOCK)


def attend_kernel(first, q_ref, k_ref, v_ref, col_ref, row_ref, out_ref, *prob_refs):
    size = k_ref.shape[1]
    group = q_ref.shape[1] // size
    for number, prob_ref in enumerate(prob_refs):
        begin = (first + number) * BLOCK
        reach = begin + BLOCK
        rows = slice(number * BLOCK, (number + 1) * BLOCK)
        here = lax.broadcasted_iota(jnp.int32, (BLOCK, reach), 0) + begin
        there = lax.broadcasted_iota(jnp.int32, (BLOCK, reach), 1)
        allowed = (col_ref[rows, :] == row_ref[:, :reach]) & (there <= here)
        bias = jnp.where(allowed, 0.0, -1e30)
        queries = q_ref[rows, :]
        for head in range(group):
            cols = slice(head * size, (head + 1) * size)
            expo = jnp.exp(dot_nt(queries[:, cols], k_ref[:reach, :]) + bias)
            share = 1.0 / jnp.sum(expo, -1, keepdims=True)
            probs = (expo * share).astype(jnp.bfloat16)
            prob_ref[0, head * BLOCK : (head + 1) * BLOCK, :] = probs
            out_ref[rows, cols] = dot_nn(probs, v_ref[:reach, :]).astype(jnp.bfloat16)


def attend(queries, keys, values, seg_ids, part, parts):
    count = queries.shape[0]
    size = 128
    heads = keys.shape[1] // size
    group = queries.shape[1] // keys.shape[1]
    rows = count // parts
    blocks = rows // BLOCK
    first = part * blocks
    reach = (part + 1) * rows
    spans = [(first + i + 1) * BLOCK for i in range(blocks)]
    return pl.pallas_call(
        functools.partial(attend_kernel, first),
        grid=(heads,),
        in_specs=[
            pl.BlockSpec((rows, group * size), lambda g: (part, g)),
            pl.BlockSpec((reach, size), lambda g: (0, g)),
            pl.BlockSpec((reach, size), lambda g: (0, g)),
            pl.BlockSpec((rows, 1), lambda g: (part, 0)),
            pl.BlockSpec((1, reach), lambda g: (0, 0)),
        ],
        out_specs=[pl.BlockSpec((rows, group * size), lambda g: (0, g))]
        + [pl.BlockSpec((1, group * BLOCK, span), lambda g: (g, 0, 0)) for span in spans],
        out_shape=[jax.ShapeDtypeStruct((rows, heads * group * size), jnp.bfloat16)]
        + [pltpu.HBM((heads, group * BLOCK, span), jnp.bfloat16) for span in spans],
        compiler_params=pltpu.CompilerParams(vmem_limit_bytes=40 * MIB),
        cost_estimate=COST,
        name="attend",
    )(hbm(queries), hbm(keys), hbm(values), seg_ids[:, None], seg_ids[None, :])


def attend_back_kernel(blocks, *refs):
    core_ref, g_ref, q_ref, k_ref, v_ref, ql_ref, kl_ref, cos_ref, sin_ref, qg_ref, kg_ref = refs[:11]
    prob_refs = refs[11 : 11 + blocks]
    dq_out, dk_out, dv_out, gains_ref, dk_ref, dv_ref = refs[-6:]
    size = k_ref.shape[1]
    group = q_ref.shape[1] // size

    def turned_back(value, rows):
        value = value.astype(jnp.bfloat16).astype(jnp.float32)
        return value * cos_ref[rows, :] - pltpu.roll(value, size // 2, 1) * sin_ref[rows, :]

    def unnorm(grad, lin, gain):
        factor = lax.rsqrt(row_mean(lin * lin) + EPS)
        hat = lin * factor
        scaled = grad * gain
        back = factor * (scaled - hat * row_mean(scaled * hat))
        return back.astype(jnp.bfloat16), jnp.sum(grad * hat, 0, keepdims=True)

    dk_ref[...] = jnp.zeros_like(dk_ref)
    dv_ref[...] = jnp.zeros_like(dv_ref)
    q_sum = jnp.zeros((1, size), jnp.float32)
    for number in range(blocks):
        rows = slice(number * BLOCK, (number + 1) * BLOCK)
        reach = (number + 1) * BLOCK
        for head in range(group):
            cols = slice(head * size, (head + 1) * size)
            grad = g_ref[placed(number, core_ref), cols]
            probs = prob_refs[number][0, head * BLOCK : (head + 1) * BLOCK, :]
            d_probs = dot_nt(grad, v_ref[:reach, :])
            probs_wide = probs.astype(jnp.float32)
            both = probs_wide * d_probs
            d_scores = (both - probs_wide * jnp.sum(both, -1, keepdims=True)).astype(jnp.bfloat16)
            dv_ref[:reach, :] += dot_tn(probs, grad)
            dk_ref[:reach, :] += dot_tn(d_scores, q_ref[rows, cols])
            d_query = dot_nn(d_scores, k_ref[:reach, :])
            turned = turned_back(d_query, rows)
            back, total = unnorm(turned * size ** (-0.5), ql_ref[rows, cols], qg_ref[...])
            dq_out[rows, cols] = back
            q_sum = q_sum + total
    turned = turned_back(dk_ref[...], slice(None))
    back, k_sum = unnorm(turned, kl_ref[...], kg_ref[...])
    dk_out[...] = back
    dv_out[...] = dv_ref[...].astype(jnp.bfloat16)
    gains_ref[0:1, :] = q_sum
    gains_ref[1:2, :] = k_sum
    gains_ref[2:, :] = jnp.zeros((6, size), jnp.float32)


def attend_back(core, grad, queries, keys, values, q_lin, k_lin, cosine, sine, q_gain, k_gain, probs, g, before):
    count = queries.shape[0]
    size = cosine.shape[1]
    group = queries.shape[1] // keys.shape[1]
    blocks = len(probs)

    def cols(width):
        return pl.BlockSpec((count, width), lambda i: (0, g))

    def whole(rows):
        return pl.BlockSpec((rows, size), lambda i: (0, 0))

    return pl.pallas_call(
        functools.partial(attend_back_kernel, blocks),
        grid=(1,),
        in_specs=[
            pl.BlockSpec(memory_space=pltpu.SMEM),
            cols(group * size), cols(group * size), cols(size), cols(size), cols(group * size),
            cols(size), whole(count), whole(count), whole(1), whole(1),
        ]
        + [pl.BlockSpec((1, *p.shape[1:]), lambda i: (g, 0, 0)) for p in probs]
        + [pl.BlockSpec(memory_space=pl.ANY)] * len(before),
        out_specs=[cols(group * size), cols(size), cols(size), whole(8)],
        out_shape=[
            jax.ShapeDtypeStruct(queries.shape, jnp.bfloat16),
            jax.ShapeDtypeStruct(keys.shape, jnp.bfloat16),
            jax.ShapeDtypeStruct(keys.shape, jnp.bfloat16),
            jax.ShapeDtypeStruct((8, size), jnp.float32),
        ],
        input_output_aliases={11 + blocks + i: i for i in range(len(before))},
        scratch_shapes=[pltpu.VMEM((count, size), jnp.float32)] * 2,
        compiler_params=pltpu.CompilerParams(vmem_limit_bytes=40 * MIB),
        cost_estimate=COST,
        name="attend_back",
    )(
        core, grad, hbm(queries), hbm(keys), hbm(values), hbm(q_lin), hbm(k_lin), cosine, sine,
        q_gain[None, :], k_gain[None, :], *[hbm(p) for p in probs], *before,
    )


def feed_kernel(count, *refs):
    lefts, (wg_ref, wu_ref, dh_ref) = refs[:count], refs[count : count + 3]
    inner_ref, hidden_ref, dg_ref, du_ref = refs[-4:]
    inner = jnp.concatenate([ref[...] for ref in lefts], 0)

    @pl.when(pl.program_id(0) == 0)
    def _():
        inner_ref[...] = inner

    gate = dot_nn(inner, wg_ref[...])
    up = dot_nn(inner, wu_ref[...])
    sig = 1.0 / (1.0 + jnp.exp(-gate))
    silu = gate * sig
    d_hidden = dh_ref[...].astype(jnp.float32)
    hidden_ref[...] = (silu * up).astype(jnp.bfloat16)
    du_ref[...] = (d_hidden * silu).astype(jnp.bfloat16)
    dg_ref[...] = (d_hidden * up * (sig + silu * (1.0 - sig))).astype(jnp.bfloat16)


def feed(first, others, w_gate, w_up, d_hidden, part, before, cols=768):
    lefts = [first, *others]
    rows, width = sum(left.shape[0] for left in lefts), first.shape[1]
    count, units = d_hidden.shape
    here = pl.BlockSpec((rows, width), lambda j: (part, 0))
    block = pl.BlockSpec((rows, cols), lambda j: (part, j))
    weight = pl.BlockSpec((width, cols), lambda j: (0, j))
    out = pltpu.HBM((count, units), jnp.bfloat16)
    return pl.pallas_call(
        functools.partial(feed_kernel, len(lefts)),
        grid=(units // cols,),
        in_specs=[pl.BlockSpec(left.shape, lambda j: (0, 0)) for left in lefts]
        + [weight, weight, block]
        + [pl.BlockSpec(memory_space=pl.ANY)] * len(before),
        out_specs=[here, block, block, block],
        out_shape=[pltpu.HBM((count, width), jnp.bfloat16), out, out, out],
        input_output_aliases={len(lefts) + 3 + i: i for i in range(len(before))},
        compiler_params=pltpu.CompilerParams(vmem_limit_bytes=40 * MIB),
        cost_estimate=COST,
        name="feed",
    )(*lefts, hbm(w_gate), hbm(w_up), hbm(d_hidden), *[hbm(array) for array in before])


ROWS = 128


def rows_call(kernel, name, rows, ins, outs):
    def spec(shape):
        if shape[0] == rows:
            return pl.BlockSpec((ROWS, shape[1]), lambda i: (i, 0))
        return pl.BlockSpec(shape, lambda i: (0, 0))

    return pl.pallas_call(
        kernel,
        grid=(rows // ROWS,),
        in_specs=[spec(a.shape) for a in ins],
        out_specs=[spec(o.shape) for o in outs],
        out_shape=outs,
        compiler_params=pltpu.CompilerParams(vmem_limit_bytes=24 * MIB),
        cost_estimate=COST,
        name=name,
    )(*ins)


def wide(ref):
    return ref[...].astype(jnp.float32)


def settle_kernel(x_ref, near_ref, far_ref, gain_ref, resid_ref, *inner_refs):
    resid = wide(x_ref) + (wide(near_ref) + wide(far_ref))
    resid_ref[...] = resid
    factor = lax.rsqrt(row_mean(resid * resid) + EPS)
    inner = (resid * factor * gain_ref[...]).astype(jnp.bfloat16)
    for j, inner_ref in enumerate(inner_refs):

        @pl.when(pl.program_id(0) == j)
        def _():
            inner_ref[...] = inner


def settle(x, near, far, gain):
    rows, width = x.shape
    pieces = rows // ROWS
    block = pl.BlockSpec((ROWS, width), lambda i: (i, 0))
    return pl.pallas_call(
        settle_kernel,
        grid=(pieces,),
        in_specs=[block, block, block, pl.BlockSpec((1, width), lambda i: (0, 0))],
        out_specs=[block] + [pl.BlockSpec((ROWS, width), lambda i: (0, 0))] * pieces,
        out_shape=[jax.ShapeDtypeStruct((rows, width), jnp.float32)]
        + [jax.ShapeDtypeStruct((ROWS, width), jnp.bfloat16)] * pieces,
        compiler_params=pltpu.CompilerParams(vmem_limit_bytes=24 * MIB),
        cost_estimate=COST,
        name="settle",
    )(x, near, far, gain[None, :])


def unsettle_kernel(near_ref, far_ref, resid_ref, grad_ref, gain_ref, out_ref, low_ref, sum_ref):
    resid = resid_ref[...].astype(jnp.float32)
    factor = lax.rsqrt(row_mean(resid * resid) + EPS)
    hat = resid * factor
    d_inner = wide(near_ref) + wide(far_ref)
    both = d_inner * hat
    scaled = d_inner * gain_ref[...]
    back = wide(grad_ref) + factor * (scaled - hat * row_mean(both * gain_ref[...]))
    out_ref[...] = back.astype(out_ref.dtype)
    if low_ref is not None:
        low_ref[...] = back.astype(jnp.bfloat16)

        @pl.when(pl.program_id(0) == 0)
        def _():
            sum_ref[...] = jnp.zeros_like(sum_ref)

        sum_ref[0:1, :] += jnp.sum(both, 0, keepdims=True)


def last_kernel(near_ref, far_ref, resid_ref, grad_ref, gain_ref, out_ref):
    unsettle_kernel(near_ref, far_ref, resid_ref, grad_ref, gain_ref, out_ref, None, None)


def unsettle(near, far, resid, grad, gain):
    rows, width = near.shape
    return rows_call(
        unsettle_kernel, "unsettle", rows, (near, far, resid, grad, gain[None, :]),
        [
            jax.ShapeDtypeStruct((rows, width), jnp.float32),
            jax.ShapeDtypeStruct((rows, width), jnp.bfloat16),
            jax.ShapeDtypeStruct((8, width), jnp.float32),
        ],
    )


def unsettle_last(near, far, resid, grad, gain):
    rows, width = near.shape
    return rows_call(
        last_kernel, "unsettle_last", rows, (near, far, resid, grad, gain[None, :]),
        [jax.ShapeDtypeStruct((rows, width), jnp.bfloat16)],
    )[0]


def live_rows_kernel(core_ref, value_ref, seg_ref, out_ref):
    out_ref[...] = jnp.where(seg_ref[...] >= 0, value_ref[...].astype(jnp.float32), 0.0).astype(jnp.bfloat16)


def live_rows(core, value, seg_ids):
    count, width = value.shape

    def from_block(i, core_ref):
        return (i ^ core_ref[0], 0)

    return pl.pallas_call(
        live_rows_kernel,
        grid_spec=pltpu.PrefetchScalarGridSpec(
            num_scalar_prefetch=1,
            grid=(count // BLOCK,),
            in_specs=[pl.BlockSpec((BLOCK, width), from_block), pl.BlockSpec((BLOCK, 1), from_block)],
            out_specs=pl.BlockSpec((BLOCK, width), lambda i, core_ref: (i, 0)),
        ),
        out_shape=jax.ShapeDtypeStruct((count, width), jnp.bfloat16),
        compiler_params=pltpu.CompilerParams(vmem_limit_bytes=24 * MIB),
        cost_estimate=COST,
        name="live_rows",
    )(core, value, seg_ids[:, None])


def ring_of(n):
    order = list(range(0, n, 2)) + [i for i in range(n - 1, 0, -1) if i % 2]
    place = [0] * n
    for spot, index in enumerate(order):
        place[index] = spot
    ahead = tuple((order[i], order[(i + 1) % n]) for i in range(n))
    back = tuple((b, a) for a, b in ahead)
    return order, place, ahead, back


def ring_table(n):
    order, place, _, _ = ring_of(n)
    table = [
        [[order[(place[i] - 1 - s) % n], order[(place[i] + 1 + s) % n]] for s in range(n)]
        for i in range(n)
    ]
    return jnp.asarray(np.array(table, np.int32).reshape(n, 2 * n))[lax.axis_index("dp")]


def ring_first(value_a, value_b, out_a_ref, out_b_ref):
    out_a_ref[...] = value_a.astype(jnp.bfloat16)
    out_b_ref[...] = value_b.astype(jnp.bfloat16)


def ring_last(turned, value_a, value_b, *out_refs):
    whole = jnp.concatenate([value_a, value_b], 1)
    begin, rows = 0, out_refs[0].shape[1 if turned[0] else 0]
    for flag, ref in zip(turned, out_refs):
        width = ref.shape[0] if flag else ref.shape[1]
        part = whole[:rows, begin : begin + width]
        ref[...] = part.T if flag else part
        begin += width
    if len(out_refs) > len(turned):
        out_refs[-1][...] = whole[rows:, :]


def ring_sum_call(finish, name, came, part, out_shape):
    def kernel(came_a_ref, came_b_ref, a_ref, b_ref, *out_refs):
        finish(wide(came_a_ref) + wide(a_ref), wide(came_b_ref) + wide(b_ref), *out_refs)

    vmem = pl.BlockSpec(memory_space=pltpu.VMEM)
    return pl.pallas_call(
        kernel,
        in_specs=[vmem] * 4,
        out_specs=jax.tree.map(lambda o: vmem, out_shape),
        out_shape=out_shape,
        compiler_params=pltpu.CompilerParams(vmem_limit_bytes=16 * MIB),
        cost_estimate=COST,
        name=name,
    )(*came, *part)


EXTRA = 16


def ring_call(finish, name, n, where, step, came, source, out_shape):
    sizes, half = [part.shape[0] // n for part in source], source[0].shape[1] // 2
    outs = len(jax.tree.leaves(out_shape))

    def kernel(where_ref, *refs):
        came_refs, part_refs = refs[: len(came)], refs[len(came) :][: len(source)]
        out_refs, owns, sem = refs[len(came) + len(source) :][:outs], refs[-3:-1], refs[-1]
        copies = []
        for side, own in enumerate(owns):
            row = 0
            for size, part_ref in zip(sizes, part_refs):
                begin = pl.multiple_of(where_ref[2 * step + side] * size, size)
                copies.append(
                    pltpu.make_async_copy(
                        part_ref.at[pl.ds(begin, size), pl.ds(side * half, half)],
                        own.at[pl.ds(row, size), :],
                        sem.at[len(copies)],
                    )
                )
                row += size
        for copy in copies:
            copy.start()
        for copy in copies:
            copy.wait()
        values = [wide(own) for own in owns]
        if came:
            values = [value + wide(ref) for value, ref in zip(values, came_refs)]
        finish(*values, *out_refs)

    return pl.pallas_call(
        kernel,
        in_specs=[pl.BlockSpec(memory_space=pltpu.SMEM)]
        + [pl.BlockSpec(memory_space=pltpu.VMEM)] * len(came)
        + [pl.BlockSpec(memory_space=pltpu.HBM)] * len(source),
        out_specs=jax.tree.map(lambda o: pl.BlockSpec(memory_space=pltpu.VMEM), out_shape),
        out_shape=out_shape,
        scratch_shapes=[pltpu.VMEM((sum(sizes), half), jnp.bfloat16)] * 2
        + [pltpu.SemaphoreType.DMA((2 * len(source),))],
        compiler_params=pltpu.CompilerParams(vmem_limit_bytes=16 * MIB),
        cost_estimate=COST,
        name=name,
    )(where, *came, *[hbm(part) for part in source])


def ring_sides(groups):
    half = sum(right.shape[1] for _, rights in groups for right in rights) // 2
    sides, filled, number = ([], []), 0, 0
    for group, (_, rights) in enumerate(groups):
        for right in rights:
            begin = 0
            while begin < right.shape[1]:
                side = filled // half
                width = min(right.shape[1] - begin, (side + 1) * half - filled)
                sides[side].append((group, number, begin, width))
                begin += width
                filled += width
            number += 1
    return sides, half


def ring_mm_call(finish, name, n, where, step, came, groups, out_shape):
    lefts = [left for group, _ in groups for left in group]
    rights = [right for _, group in groups for right in group]
    count = sum(left.shape[0] for left in groups[0][0])
    size = lefts[0].shape[1] // n
    sides, half = ring_sides(groups)
    outs = len(jax.tree.leaves(out_shape))
    used = [sorted({term[0] for term in side}) for side in sides]

    def kernel(where_ref, *refs):
        came_refs, refs = refs[: len(came)], refs[len(came) :]
        left_refs, refs = refs[: len(lefts)], refs[len(lefts) :]
        right_refs, refs = refs[: len(rights)], refs[len(rights) :]
        out_refs, refs = refs[:outs], refs[outs:]
        right_bufs, left_bufs, sem = refs[:2], list(refs[2:-1]), refs[-1]
        waits, chunks = ([], []), ({}, {})
        for side in range(2):
            begin = pl.multiple_of(where_ref[2 * step + side] * size, size)
            at = 0
            for group in used[side]:
                buffer = left_bufs.pop(0)
                chunks[side][group] = buffer
                first = sum(len(g[0]) for g in groups[:group])
                row = 0
                for ref in left_refs[first : first + len(groups[group][0])]:
                    rows = ref.shape[0]
                    copy = pltpu.make_async_copy(
                        ref.at[:, pl.ds(begin, size)], buffer.at[pl.ds(row, rows), :], sem.at[side]
                    )
                    copy.start()
                    waits[side].append(copy)
                    row += rows
            for _, number, column, width in sides[side]:
                copy = pltpu.make_async_copy(
                    right_refs[number].at[:, pl.ds(column, width)],
                    right_bufs[side].at[:, pl.ds(at, width)],
                    sem.at[side],
                )
                copy.start()
                waits[side].append(copy)
                at += width
        values = []
        for side in range(2):
            for copy in waits[side]:
                copy.wait()
            products, at = [], 0
            for group in used[side]:
                width = sum(term[3] for term in sides[side] if term[0] == group)
                products.append(
                    dot_tn(chunks[side][group][...], right_bufs[side][:, at : at + width])
                )
                at += width
            value = jnp.concatenate(products, 1) if len(products) > 1 else products[0]
            values.append(value + wide(came_refs[side]) if came else value)
        finish(*values, *out_refs)

    return pl.pallas_call(
        kernel,
        in_specs=[pl.BlockSpec(memory_space=pltpu.SMEM)]
        + [pl.BlockSpec(memory_space=pltpu.VMEM)] * len(came)
        + [pl.BlockSpec(memory_space=pltpu.HBM)] * (len(lefts) + len(rights)),
        out_specs=jax.tree.map(lambda o: pl.BlockSpec(memory_space=pltpu.VMEM), out_shape),
        out_shape=out_shape,
        scratch_shapes=[pltpu.VMEM((count, half), jnp.bfloat16)] * 2
        + [pltpu.VMEM((count, size), jnp.bfloat16)] * (len(used[0]) + len(used[1]))
        + [pltpu.SemaphoreType.DMA((2,))],
        compiler_params=pltpu.CompilerParams(vmem_limit_bytes=32 * MIB),
        cost_estimate=COST,
        name=name,
    )(where, *came, *[hbm(i) for i in lefts + rights])


class Order:
    def __init__(self):
        self.last = None

    def run(self, piece, first, *rest):
        if self.last is not None:
            first, _ = lax.optimization_barrier((first, self.last))
        out = piece(first, *rest)
        self.last = jax.tree.leaves(out)[0]
        return out


    def tie(self, value):
        return lax.optimization_barrier((value, self.last))[0]


class Ring:
    def __init__(self, n, where, order, groups, ahead_made, turned, last_shapes):
        self.n, self.where, self.order = n, where, order
        self.last, self.last_shapes = functools.partial(ring_last, turned), last_shapes
        self.step_no = 0
        _, _, self.ahead, self.back = ring_of(n)
        size = groups[0][0][0].shape[1] // n
        half = sum(right.shape[1] for _, rights in groups for right in rights) // 2
        self.ahead_made = ahead_made and size % 128 == 0
        if self.ahead_made:
            self.piece, self.source = ring_mm_call, groups
        else:
            (lefts, (first, *others)), *more = groups
            self.piece = ring_call
            self.source = [order.run(lambda r: weight_grad([(lefts, [r, *others]), *more]), first)]
        self.out = [jax.ShapeDtypeStruct((size, half), jnp.bfloat16)] * 2

    def add(self, extra):
        self.source.append(extra)
        rows, half = self.out[0].shape
        self.out = [jax.ShapeDtypeStruct((rows + EXTRA, half), jnp.bfloat16)] * 2
        self.last_shapes = [*self.last_shapes, jax.ShapeDtypeStruct((EXTRA, 2 * half), jnp.float32)]

    def begin(self):
        self.send(self.make(0))

    def make(self, step):
        return self.order.run(
            lambda w: self.piece(
                ring_first, "ring_first", self.n, w, step, (), self.source, self.out
            ),
            self.where,
        )

    def call(self, finish, name, out):
        if self.ahead_made:
            return self.order.run(
                lambda a: ring_sum_call(finish, name, (a, self.came[1]), self.part, out), self.came[0]
            )
        return self.order.run(
            lambda a: self.piece(
                finish, name, self.n, self.where, self.step_no, (a, self.came[1]), self.source, out
            ),
            self.came[0],
        )

    def send(self, held):
        self.came = (lax.ppermute(held[0], "dp", self.ahead), lax.ppermute(held[1], "dp", self.back))

    def prepare(self):
        if self.ahead_made and self.step_no < self.n - 1:
            self.part = self.make(self.step_no + 1)

    def step(self):
        if self.step_no < self.n - 1:
            self.step_no += 1
            if self.step_no < self.n - 1:
                self.send(self.call(ring_first, "ring_add", self.out))
            else:
                self.result = self.call(self.last, "ring_last", self.last_shapes)


DOTS = {"nn": dot_nn, "nt": dot_nt, "tn": dot_tn}


def pairs_kernel(kind, outs, count, weighed, core_ref, *refs):
    out_refs = refs[-len(outs) - weighed :]
    if weighed:
        sums = jnp.zeros((1, out_refs[-1].shape[1]), jnp.float32)
    for (spots, _), out_ref in zip(outs, out_refs):
        for i, spot in enumerate(spots):
            if spot < 0:
                rows = pl.ds(pl.multiple_of(((-1 - spot) ^ core_ref[0]) * BLOCK, BLOCK), BLOCK)
            else:
                rows = slice(spot * BLOCK, (spot + 1) * BLOCK)
            total = None
            for left_ref, right_ref in zip(refs[: 2 * count : 2], refs[1 : 2 * count : 2]):
                value = DOTS[kind](left_ref[rows, :], right_ref[...])
                total = value if total is None else total + value
            out_ref[i * BLOCK : (i + 1) * BLOCK, :] = total.astype(out_ref.dtype)
            if weighed:
                sums += jnp.sum(total * wide_at(refs[2 * count], rows), 0, keepdims=True)
    if weighed:
        out_refs[-1][...] = jnp.broadcast_to(sums, out_refs[-1].shape)


def wide_at(ref, rows):
    return ref[rows, :].astype(jnp.float32)


def pairs(core, kind, terms, outs, part=0, parts=1, before=(), weights=None, cols=512):
    width = terms[0][1].shape[1 if kind == "nn" else 0]
    steps = width // cols // parts
    begin = part * steps
    ins, specs = [], []
    for left, right in terms:
        ins += [left, right]
        specs.append(pl.BlockSpec(left.shape, lambda j: (0, 0)))
        if kind == "nn":
            specs.append(pl.BlockSpec((right.shape[0], cols), lambda j: (0, begin + j)))
        else:
            specs.append(pl.BlockSpec((cols, right.shape[1]), lambda j: (begin + j, 0)))
    shapes = [(len(o[0]) * BLOCK, o[1]) for o in outs]
    weighed = weights is not None
    if weighed:
        ins.append(weights)
        specs.append(pl.BlockSpec((weights.shape[0], cols), lambda j: (0, begin + j)))
        shapes.append((8, jnp.float32))
    return pl.pallas_call(
        functools.partial(pairs_kernel, kind, outs, len(terms), int(weighed)),
        grid=(steps,),
        in_specs=[pl.BlockSpec(memory_space=pltpu.SMEM)]
        + specs
        + [pl.BlockSpec(memory_space=pl.ANY)] * len(before),
        out_specs=[pl.BlockSpec((rows, cols), lambda j: (0, begin + j)) for rows, _ in shapes],
        out_shape=[jax.ShapeDtypeStruct((rows, width), kind) for rows, kind in shapes],
        input_output_aliases={1 + len(ins) + i: i for i in range(len(before))},
        compiler_params=pltpu.CompilerParams(vmem_limit_bytes=40 * MIB),
        cost_estimate=COST,
        name="pairs",
    )(core, *[hbm(i) for i in ins], *before)


def split_pair_kernel(core_ref, left_ref, right_ref, mine_ref, *other_refs):
    for spot, own in ((1, False), (0, True)):
        rows = pl.ds(pl.multiple_of((spot ^ core_ref[0]) * BLOCK, BLOCK), BLOCK)
        value = dot_nn(left_ref[rows, :], right_ref[...])
        if own:
            mine_ref[...] = value
        else:
            for j, ref in enumerate(other_refs):
                ref[...] = value[j * ROWS : (j + 1) * ROWS, :].astype(jnp.bfloat16)


def split_pair(core, left, right, cols=512):
    width = right.shape[1]

    def block(rows):
        return pl.BlockSpec((rows, cols), lambda j: (0, j))

    pieces = BLOCK // ROWS
    return pl.pallas_call(
        split_pair_kernel,
        grid=(width // cols,),
        in_specs=[
            pl.BlockSpec(memory_space=pltpu.SMEM),
            pl.BlockSpec(left.shape, lambda j: (0, 0)),
            block(right.shape[0]),
        ],
        out_specs=[block(BLOCK)] + [block(ROWS)] * pieces,
        out_shape=[jax.ShapeDtypeStruct((BLOCK, width), jnp.float32)]
        + [jax.ShapeDtypeStruct((ROWS, width), jnp.bfloat16)] * pieces,
        compiler_params=pltpu.CompilerParams(vmem_limit_bytes=24 * MIB),
        cost_estimate=COST,
        name="split_pair",
    )(core, left, right)


def near_kernel(mine_ref, *refs):
    out_ref = refs[-1]
    for j, came_ref in enumerate(refs[:-1]):

        @pl.when(pl.program_id(0) == j)
        def _():
            out_ref[...] = (mine_ref[...] + wide(came_ref)).astype(jnp.bfloat16)


def near_add(first, others, mine):
    came = [first, *others]
    rows, width = came[0].shape
    block = pl.BlockSpec((rows, width), lambda i: (i, 0))
    return pl.pallas_call(
        near_kernel,
        grid=(len(came),),
        in_specs=[block] + [pl.BlockSpec((rows, width), lambda i: (0, 0))] * len(came),
        out_specs=block,
        out_shape=jax.ShapeDtypeStruct(mine.shape, jnp.bfloat16),
        compiler_params=pltpu.CompilerParams(vmem_limit_bytes=24 * MIB),
        cost_estimate=COST,
        name="near_add",
    )(mine, *came)


def mixed_kernel(resid_ref, near_ref, far_ref, out_ref):
    out_ref[...] = (resid_ref[...] + (wide(near_ref) + wide(far_ref))).astype(jnp.bfloat16)


def nt_kernel(*refs):
    out_ref = refs[-1]
    begin = 0
    for left_ref in refs[1:-1]:
        rows = slice(begin, begin + left_ref.shape[0])
        out_ref[rows, :] = dot_nt(left_ref[...], refs[0][...]).astype(jnp.bfloat16)
        begin += left_ref.shape[0]


def times_turned(lefts, right, cols=512):
    rows = sum(left.shape[0] for left in lefts)
    return pl.pallas_call(
        nt_kernel,
        grid=(right.shape[0] // cols,),
        in_specs=[pl.BlockSpec((cols, right.shape[1]), lambda j: (j, 0))]
        + [pl.BlockSpec(left.shape, lambda j: (0, 0)) for left in lefts],
        out_specs=pl.BlockSpec((rows, cols), lambda j: (0, j)),
        out_shape=pltpu.HBM((rows, right.shape[0]), jnp.bfloat16),
        compiler_params=pltpu.CompilerParams(vmem_limit_bytes=40 * MIB),
        cost_estimate=COST,
        name="times_turned",
    )(right, *lefts)


def weight_grad_kernel(counts, *refs):
    out_ref = refs[-1]
    at, begin = 0, 0
    for lefts, rights in counts:
        left = refs[at][...]
        if lefts > 1:
            left = jnp.concatenate([ref[...] for ref in refs[at : at + lefts]], 0)
        for ref in refs[at + lefts : at + lefts + rights]:
            width = ref.shape[1]
            out_ref[:, begin : begin + width] = dot_tn(left, ref[...]).astype(jnp.bfloat16)
            begin += width
        at += lefts + rights


def weight_grad(groups, rows=256):
    width = groups[0][0][0].shape[1]
    ins, specs, cols = [], [], 0
    for lefts, rights in groups:
        ins += [*lefts, *rights]
        specs += [pl.BlockSpec((left.shape[0], rows), lambda i: (0, i)) for left in lefts]
        specs += [pl.BlockSpec(right.shape, lambda i: (0, 0)) for right in rights]
        cols += sum(right.shape[1] for right in rights)
    return pl.pallas_call(
        functools.partial(weight_grad_kernel, [(len(a), len(b)) for a, b in groups]),
        grid=(width // rows,),
        in_specs=specs,
        out_specs=pl.BlockSpec((rows, cols), lambda i: (i, 0)),
        out_shape=jax.ShapeDtypeStruct((width, cols), jnp.bfloat16),
        compiler_params=pltpu.CompilerParams(vmem_limit_bytes=32 * MIB),
        cost_estimate=COST,
        name="weight_grad",
    )(*[hbm(i) for i in ins])


def join_kernel(core_ref, mine_ref, *refs):
    out_ref = refs[-1]

    @pl.when(pl.program_id(0) % 2 == 0)
    def _():
        out_ref[...] = mine_ref[...]

    for j, other_ref in enumerate(refs[:-1]):

        @pl.when(pl.program_id(0) == 2 * j + 1)
        def _():
            out_ref[...] = other_ref[...]


def join(first, others, core, mine):
    rows, width = mine.shape
    came = [first, *others]
    return pl.pallas_call(
        join_kernel,
        grid_spec=pltpu.PrefetchScalarGridSpec(
            num_scalar_prefetch=1,
            grid=(2 * rows // BLOCK,),
            in_specs=[pl.BlockSpec((BLOCK, width), lambda i, core_ref: (i >> 1, 0))]
            + [pl.BlockSpec((BLOCK, width), lambda i, core_ref: (0, 0))] * len(came),
            out_specs=pl.BlockSpec((BLOCK, width), lambda i, core_ref: (i ^ core_ref[0], 0)),
        ),
        out_shape=jax.ShapeDtypeStruct((2 * rows, width), mine.dtype),
        compiler_params=pltpu.CompilerParams(vmem_limit_bytes=24 * MIB),
        cost_estimate=COST,
        name="join",
    )(core, mine, *came)


def cut_up(value, pieces, swap):
    share = value.shape[0] // pieces
    return [
        lax.ppermute(value[i * share : (i + 1) * share], "tensor", swap) for i in range(pieces)
    ]


def to_core(value):
    return lax.ppermute(value, "tensor", CORE_SWAP)


def to_chip(value):
    return lax.ppermute(value, "tensor", CHIP_SWAP)


def low(value):
    return value.astype(jnp.bfloat16)


def on_device(
    n, tokens, seg_ids, cotangent, attn_gain, w_query, w_key, w_value, w_out, mlp_gain, w_gate, w_up,
    w_down, query_gain, key_gain,
):
    count, width = tokens.shape
    size = query_gain.shape[0]
    parts = 2
    rows = count // parts
    core_no = lax.axis_index("tensor") % 2
    core = core_no.astype(jnp.int32)[None]
    where = ring_table(n)
    order = Order()
    run = order.run

    def both_parts(piece):
        return [piece(j) for j in range(parts)]

    def own_rows(value, part, other=0):
        begin = part * rows + (core_no ^ other) * BLOCK
        return lax.dynamic_slice_in_dim(value, begin, BLOCK, 0)

    index = jnp.arange(count, dtype=jnp.int32)
    place = jnp.where(seg_ids >= 0, index - seg_ids, index).astype(jnp.float32)
    freq = THETA ** (-(jnp.arange(size // 2, dtype=jnp.float32) * 2.0) / size)
    turn = place[:, None] * freq[None, :]
    cosine, sine = jnp.cos(turn), jnp.sin(turn)
    cosine, sine = jnp.concatenate([cosine, cosine], -1), jnp.concatenate([-sine, sine], -1)

    normed, queries, keys, values, q_lin, k_lin = run(
        front, tokens, attn_gain, w_query, w_key, w_value, cosine, sine, query_gain, key_gain
    )
    wide_low = (jnp.float32, jnp.bfloat16)

    def mine_other(mine, other):
        return ((mine, wide_low[0]), (other, wide_low[1]))

    attended, probs, near, far = [], [], [], []
    for j in range(parts):
        out = run(lambda q: attend(q, keys, values, seg_ids, j, parts), queries)
        attended.append(out[0])
        probs += out[1:]
        mine, *other = run(lambda a: split_pair(core, a, w_out), out[0])
        other = [to_core(piece) for piece in other]
        near.append(run(near_add, other[0], other[1:], mine))
        far.append(to_chip(near[j]))

    grad_low = run(lambda c: live_rows(core, c, seg_ids), cotangent)
    grad_low, where = lax.optimization_barrier((grad_low, where))
    d_hidden = run(lambda g: times_turned([g], w_down), grad_low)
    x_own = both_parts(lambda j: own_rows(tokens, j))

    resid, fed = [], ()
    for j in range(parts):
        held, *inner_own = run(lambda f: settle(x_own[j], near[j], f, mlp_gain), far[j])
        resid.append(held)
        inner_other = [to_core(piece) for piece in inner_own]
        fed = run(
            lambda o: feed(inner_own[0], [*inner_own[1:], o, *inner_other[1:]], w_gate, w_up, d_hidden, j, fed),
            inner_other[0],
        )
    inner, hidden, d_gate, d_up = fed

    def shape(*extent):
        return jax.ShapeDtypeStruct(extent, jnp.float32)

    units, share = w_gate.shape[1], width // n
    q_cols, k_cols = w_query.shape[1], w_key.shape[1]
    active, results = [], {}

    def ring(groups, ahead_made, turned, *last_shapes):
        return Ring(n, where, order, groups, ahead_made, turned, last_shapes)

    def begin(name, made):
        made.begin()
        active.append((name, made))

    def tick():
        for item in list(active):
            item[1].step()
            if item[1].step_no == n - 1:
                results[item[0]] = item[1].result
                active.remove(item)

    def prepare():
        for item in active:
            item[1].prepare()

    mlp_ring = ring(
        [([grad_low], [hidden]), ([inner], [d_gate, d_up])], True, (True, False, False),
        shape(units, share), shape(share, units), shape(share, units),
    )
    begin("mlp", mlp_ring)
    prepare()
    made = ()
    for half in range(2):
        made = run(
            lambda d: pairs(
                core, "nt", [(d, w_gate), (d_up, w_up)], mine_other((0, 2), (1, 3)), half, 2, made
            ),
            d_gate,
        )
    tick()
    came3 = cut_up(order.tie(made[1]), parts, CORE_SWAP)
    near3 = run(near_add, came3[0], came3[1:], made[0])
    far3 = to_chip(near3)
    prepare()
    mixed_mine, mixed_other = run(
        lambda h: pairs(core, "nn", [(h, w_down)], mine_other((0, 2), (1, 3))), hidden
    )
    blocks = [part[i : i + BLOCK] for part in attended for i in range(0, rows, BLOCK)]
    attended_mine_first = jnp.where(
        core_no == 0,
        jnp.concatenate(blocks, 0),
        jnp.concatenate([blocks[i ^ 1] for i in range(len(blocks))], 0),
    )
    grad_own = jnp.concatenate([grad_low[j * rows : j * rows + BLOCK] for j in range(parts)], 0)
    resid_own = jnp.concatenate(resid, 0)
    tick()
    prepare()
    tick()
    d_resid, branch_own, mlp_sums = run(
        lambda f: unsettle(near3, f, resid_own, grad_own, mlp_gain), far3
    )
    branch_other = cut_up(branch_own, parts, CORE_SWAP)
    prepare()
    d_branch = []
    for j in range(parts):
        d_branch += [branch_own[j * BLOCK : (j + 1) * BLOCK], branch_other[j]]
    d_attended = run(lambda d: times_turned([*d_branch[:-1], d], w_out), d_branch[-1])
    heads_count = k_cols // size
    d_lin, gain_sums = (), jnp.zeros((8, size), jnp.float32)
    for g in range(heads_count):
        *d_lin, total = run(
            lambda a: attend_back(
                core, a, queries, keys, values, q_lin, k_lin, cosine, sine, query_gain, key_gain,
                probs, g, d_lin,
            ),
            d_attended,
        )
        gain_sums = gain_sums + total
        if g == 0:
            tick()
            came2 = cut_up(order.tie(mixed_other), parts, CORE_SWAP)
            prepare()
    near2 = run(near_add, came2[0], came2[1:], mixed_mine)
    far2 = to_chip(near2)
    d_q_lin, d_k_lin, d_values = d_lin
    mine, other, attn_sums = run(
        lambda d: pairs(
            core, "nt", [(d, w_query), (d_k_lin, w_key), (d_values, w_value)],
            mine_other((-1, -3), (-2, -4)), weights=normed,
        ),
        d_q_lin,
    )
    gains = [0.5 * mlp_sums[0], attn_sums[0] / attn_gain, gain_sums[0], gain_sums[1]]
    gains = jnp.concatenate([part.reshape(n, -1) for part in gains], 1)
    tick()
    came4 = cut_up(order.tie(other), parts, CORE_SWAP)
    near4 = run(near_add, came4[0], came4[1:], mine)
    far4 = to_chip(near4)
    prepare()
    gains = run(jnp.add, to_core(gains), gains)
    out_value = ring(
        [(d_branch, [attended_mine_first]), ([normed], [d_values])], False, (True, False),
        shape(q_cols, share), shape(share, k_cols),
    )
    gains = run(jnp.add, to_chip(gains), gains)
    extra_cols = q_cols + k_cols
    extra = jnp.pad(low(gains), ((0, 0), (0, EXTRA * extra_cols - gains.shape[1])))
    out_value.add(extra.reshape(n * EXTRA, extra_cols))
    tick()
    mixed = run(lambda f, n_, r: rows_call(
        mixed_kernel, "mixed", n_.shape[0], (r, n_, f), [jax.ShapeDtypeStruct(n_.shape, jnp.bfloat16)]
    )[0], far2, near2, resid_own)
    mixed_far = cut_up(mixed, parts, CORE_SWAP)
    prepare()
    query_key = ring(
        [([normed], [d_q_lin, d_k_lin])], False, (False, False),
        shape(share, q_cols), shape(share, k_cols),
    )
    mixed = run(join, mixed_far[0], mixed_far[1:], core, mixed)
    tick()
    begin("out value", out_value)
    begin("query key", query_key)
    tick()
    tick()
    tick()
    grad_tokens = run(
        lambda f: unsettle_last(near4, f, jnp.concatenate(x_own, 0), d_resid, attn_gain), far4
    )
    other = cut_up(grad_tokens, parts, CORE_SWAP)
    tick()
    grad_tokens = run(join, other[0], other[1:], core, grad_tokens)
    while active:
        tick()
    grad_down, grad_gate, grad_up = results["mlp"]
    (grad_out, grad_value, extra), (grad_query, grad_key) = results["out value"], results["query key"]
    gains, begins = extra.reshape(-1), np.cumsum([0, width, width, size, size]) // n
    mlp_sum, attn_sum, q_sum, k_sum = [gains[begins[i] : begins[i + 1]] for i in range(4)]
    return (
        mixed,
        grad_tokens,
        attn_sum,
        grad_query,
        grad_key,
        grad_value,
        grad_out,
        mlp_sum,
        grad_gate,
        grad_up,
        grad_down,
        q_sum,
        k_sum,
    )


def solution(mesh):
    rows, cols = P("dp", "tensor"), P("tensor", "dp")
    return jax.shard_map(
        functools.partial(on_device, mesh.shape["dp"]),
        mesh=mesh,
        in_specs=(
            P("dp", None), P("dp"), P("dp", None), P(), P(None, "tensor"), P(None, "tensor"),
            P(None, "tensor"), P("tensor", None), P(), P(None, "tensor"), P(None, "tensor"),
            P("tensor", None), P(), P(),
        ),
        out_specs=(
            P("dp", None), P("dp", None), P("dp"), rows, rows, rows, cols, P("dp"), rows, rows, cols,
            P("dp"), P("dp"),
        ),
        check_vma=False,
    )
```

```python
import functools

import jax
import jax.numpy as jnp
import numpy as np
from jax import lax
from jax.experimental import pallas as pl
from jax.experimental.pallas import tpu as pltpu
from jax.sharding import PartitionSpec as P

EPS = 1e-06
THETA = 1000000.0
CORE_SWAP = ((0, 1), (1, 0), (2, 3), (3, 2))
CHIP_SWAP = ((0, 2), (1, 3), (2, 0), (3, 1))
BLOCK = 256
MIB = 1024 * 1024
COST = pl.CostEstimate(flops=0, bytes_accessed=0, transcendentals=0)


def dot_nn(left, right):
    return jnp.dot(left, right, preferred_element_type=jnp.float32)


def dot_nt(left, right):
    return lax.dot_general(
        left, right, (((1,), (1,)), ((), ())), preferred_element_type=jnp.float32
    )


def dot_tn(left, right):
    return lax.dot_general(
        left, right, (((0,), (0,)), ((), ())), preferred_element_type=jnp.float32
    )

SENDS = {
    "core3": CORE_SWAP,
    "x3": CHIP_SWAP,
    "core2": CORE_SWAP,
    "x2": CHIP_SWAP,
    "coreM": CORE_SWAP,
    "coreB": CORE_SWAP,
    "gains1": CORE_SWAP,
    "gains2": CHIP_SWAP,
    "core4": CORE_SWAP,
    "x4": CHIP_SWAP,
    "coreG": CORE_SWAP,
}
TIES = {
    "coreM": ("lp", 1),
    "x4": ("add", 6),
    "core2": ("add", 2),
}
SCHEDULE = (
    "piece0", "dih0", "dih1", "piece", "add", "near3", "piece", "piece",
    "mixp", "add", "near2", "piece", "unsettle", "add", "piece", "datt",
    "att0", "sel", "add", "att1", "dn", "mixed", "add", "piece",
    "gc", "gx", "lp", "lf", "near4", "lp", "add", "la",
    "lp", "la", "joinM", "lp", "la", "lp", "lp", "piece",
    "la", "ul", "la", "add", "lp", "la", "joinG", "lp",
    "la",
)


def hbm(value):
    return pltpu.with_memory_space_constraint(value, pltpu.HBM)


def row_mean(value):
    return jnp.mean(value, -1, keepdims=True)


def front_kernel(
    x_ref, gain_ref, wq_ref, wk_ref, wv_ref, cos_ref, sin_ref, qg_ref, kg_ref,
    normed_ref, q_ref, k_ref, v_ref, ql_ref, kl_ref,
):
    size = cos_ref.shape[1]
    x = x_ref[...].astype(jnp.float32)
    factor = lax.rsqrt(row_mean(x * x) + EPS)
    normed = (x * factor * gain_ref[...]).astype(jnp.bfloat16)
    normed_ref[...] = normed
    cosine, sine = cos_ref[...], sin_ref[...]

    def heads(lin, gain, scale, lin_ref, out_ref):
        lin_ref[...] = lin
        for head in range(lin.shape[1] // size):
            cols = slice(head * size, (head + 1) * size)
            part = lin[:, cols]
            scaled = part * lax.rsqrt(row_mean(part * part) + EPS) * gain
            turned = scaled * cosine + pltpu.roll(scaled, size // 2, 1) * sine
            out_ref[:, cols] = (turned * scale).astype(jnp.bfloat16)

    heads(dot_nn(normed, wq_ref[...]), qg_ref[...], size ** (-0.5), ql_ref, q_ref)
    heads(dot_nn(normed, wk_ref[...]), kg_ref[...], 1.0, kl_ref, k_ref)
    v_ref[...] = dot_nn(normed, wv_ref[...]).astype(jnp.bfloat16)


def front(tokens, gain, wq, wk, wv, cosine, sine, q_gain, k_gain):
    count, width = tokens.shape
    size = cosine.shape[1]
    q_cols, k_cols = wq.shape[1], wk.shape[1]

    def rows(cols):
        return pl.BlockSpec((BLOCK, cols), lambda i: (i, 0))

    def whole(*shape):
        return pl.BlockSpec(shape, lambda i: (0,) * len(shape))

    def out(cols, kind):
        return pltpu.HBM((count, cols), kind)

    return pl.pallas_call(
        front_kernel,
        grid=(count // BLOCK,),
        in_specs=[
            rows(width), whole(1, width), whole(width, q_cols), whole(width, k_cols),
            whole(width, k_cols), rows(size), rows(size), whole(1, size), whole(1, size),
        ],
        out_specs=[rows(width), rows(q_cols), rows(k_cols), rows(k_cols), rows(q_cols), rows(k_cols)],
        out_shape=[
            out(width, jnp.bfloat16), out(q_cols, jnp.bfloat16), out(k_cols, jnp.bfloat16),
            out(k_cols, jnp.bfloat16), out(q_cols, jnp.float32), out(k_cols, jnp.float32),
        ],
        compiler_params=pltpu.CompilerParams(vmem_limit_bytes=40 * MIB),
        cost_estimate=COST,
        name="front",
    )(
        hbm(tokens), gain[None, :], hbm(wq), hbm(wk), hbm(wv), cosine, sine, q_gain[None, :],
        k_gain[None, :],
    )


def pair_rows(value, size):
    return jnp.concatenate([value[:, i : i + size] for i in range(0, value.shape[1], size)], 0)


def placed(number, core_ref):
    spot = number // 2 * 2 + (core_ref[0] ^ (number % 2))
    return pl.ds(pl.multiple_of(spot * BLOCK, BLOCK), BLOCK)


def attend_kernel(first, q_ref, k_ref, v_ref, col_ref, row_ref, out_ref, *prob_refs):
    size = k_ref.shape[1]
    group = q_ref.shape[1] // size
    for number, prob_ref in enumerate(prob_refs):
        begin = (first + number) * BLOCK
        reach = begin + BLOCK
        rows = slice(number * BLOCK, (number + 1) * BLOCK)
        here = lax.broadcasted_iota(jnp.int32, (BLOCK, reach), 0) + begin
        there = lax.broadcasted_iota(jnp.int32, (BLOCK, reach), 1)
        allowed = (col_ref[rows, :] == row_ref[:, :reach]) & (there <= here)
        bias = jnp.where(allowed, 0.0, -1e30)
        queries = q_ref[rows, :]
        for head in range(group):
            cols = slice(head * size, (head + 1) * size)
            expo = jnp.exp(dot_nt(queries[:, cols], k_ref[:reach, :]) + bias)
            share = 1.0 / jnp.sum(expo, -1, keepdims=True)
            probs = (expo * share).astype(jnp.bfloat16)
            prob_ref[0, head * BLOCK : (head + 1) * BLOCK, :] = probs
            out_ref[rows, cols] = dot_nn(probs, v_ref[:reach, :]).astype(jnp.bfloat16)


def attend(queries, keys, values, seg_ids, part, parts):
    count = queries.shape[0]
    size = 128
    heads = keys.shape[1] // size
    group = queries.shape[1] // keys.shape[1]
    rows = count // parts
    blocks = rows // BLOCK
    first = part * blocks
    reach = (part + 1) * rows
    spans = [(first + i + 1) * BLOCK for i in range(blocks)]
    return pl.pallas_call(
        functools.partial(attend_kernel, first),
        grid=(heads,),
        in_specs=[
            pl.BlockSpec((rows, group * size), lambda g: (part, g)),
            pl.BlockSpec((reach, size), lambda g: (0, g)),
            pl.BlockSpec((reach, size), lambda g: (0, g)),
            pl.BlockSpec((rows, 1), lambda g: (part, 0)),
            pl.BlockSpec((1, reach), lambda g: (0, 0)),
        ],
        out_specs=[pl.BlockSpec((rows, group * size), lambda g: (0, g))]
        + [pl.BlockSpec((1, group * BLOCK, span), lambda g: (g, 0, 0)) for span in spans],
        out_shape=[jax.ShapeDtypeStruct((rows, heads * group * size), jnp.bfloat16)]
        + [pltpu.HBM((heads, group * BLOCK, span), jnp.bfloat16) for span in spans],
        compiler_params=pltpu.CompilerParams(vmem_limit_bytes=40 * MIB),
        cost_estimate=COST,
        name="attend",
    )(hbm(queries), hbm(keys), hbm(values), seg_ids[:, None], seg_ids[None, :])


def attend_back_kernel(blocks, *refs):
    core_ref, g_ref, q_ref, k_ref, v_ref, ql_ref, kl_ref, cos_ref, sin_ref, qg_ref, kg_ref = refs[:11]
    prob_refs = refs[11 : 11 + blocks]
    dq_out, dk_out, dv_out, gains_ref, dk_ref, dv_ref = refs[-6:]
    size = k_ref.shape[1]
    group = q_ref.shape[1] // size

    def turned_back(value, rows):
        value = value.astype(jnp.bfloat16).astype(jnp.float32)
        return value * cos_ref[rows, :] - pltpu.roll(value, size // 2, 1) * sin_ref[rows, :]

    def unnorm(grad, lin, gain):
        factor = lax.rsqrt(row_mean(lin * lin) + EPS)
        hat = lin * factor
        scaled = grad * gain
        back = factor * (scaled - hat * row_mean(scaled * hat))
        return back.astype(jnp.bfloat16), jnp.sum(grad * hat, 0, keepdims=True)

    dk_ref[...] = jnp.zeros_like(dk_ref)
    dv_ref[...] = jnp.zeros_like(dv_ref)
    q_sum = jnp.zeros((1, size), jnp.float32)
    for number in range(blocks):
        rows = slice(number * BLOCK, (number + 1) * BLOCK)
        reach = (number + 1) * BLOCK
        for head in range(group):
            cols = slice(head * size, (head + 1) * size)
            grad = g_ref[placed(number, core_ref), cols]
            probs = prob_refs[number][0, head * BLOCK : (head + 1) * BLOCK, :]
            d_probs = dot_nt(grad, v_ref[:reach, :])
            probs_wide = probs.astype(jnp.float32)
            both = probs_wide * d_probs
            d_scores = (both - probs_wide * jnp.sum(both, -1, keepdims=True)).astype(jnp.bfloat16)
            dv_ref[:reach, :] += dot_tn(probs, grad)
            dk_ref[:reach, :] += dot_tn(d_scores, q_ref[rows, cols])
            d_query = dot_nn(d_scores, k_ref[:reach, :])
            turned = turned_back(d_query, rows)
            back, total = unnorm(turned * size ** (-0.5), ql_ref[rows, cols], qg_ref[...])
            dq_out[rows, cols] = back
            q_sum = q_sum + total
    turned = turned_back(dk_ref[...], slice(None))
    back, k_sum = unnorm(turned, kl_ref[...], kg_ref[...])
    dk_out[...] = back
    dv_out[...] = dv_ref[...].astype(jnp.bfloat16)
    gains_ref[0:1, :] = q_sum
    gains_ref[1:2, :] = k_sum
    gains_ref[2:, :] = jnp.zeros((6, size), jnp.float32)


def attend_back(core, grad, queries, keys, values, q_lin, k_lin, cosine, sine, q_gain, k_gain, probs, g, before):
    count = queries.shape[0]
    size = cosine.shape[1]
    group = queries.shape[1] // keys.shape[1]
    blocks = len(probs)

    def cols(width):
        return pl.BlockSpec((count, width), lambda i: (0, g))

    def whole(rows):
        return pl.BlockSpec((rows, size), lambda i: (0, 0))

    return pl.pallas_call(
        functools.partial(attend_back_kernel, blocks),
        grid=(1,),
        in_specs=[
            pl.BlockSpec(memory_space=pltpu.SMEM),
            cols(group * size), cols(group * size), cols(size), cols(size), cols(group * size),
            cols(size), whole(count), whole(count), whole(1), whole(1),
        ]
        + [pl.BlockSpec((1, *p.shape[1:]), lambda i: (g, 0, 0)) for p in probs]
        + [pl.BlockSpec(memory_space=pl.ANY)] * len(before),
        out_specs=[cols(group * size), cols(size), cols(size), whole(8)],
        out_shape=[
            pltpu.HBM(queries.shape, jnp.bfloat16),
            pltpu.HBM(keys.shape, jnp.bfloat16),
            pltpu.HBM(keys.shape, jnp.bfloat16),
            jax.ShapeDtypeStruct((8, size), jnp.float32),
        ],
        input_output_aliases={11 + blocks + i: i for i in range(len(before))},
        scratch_shapes=[pltpu.VMEM((count, size), jnp.float32)] * 2,
        compiler_params=pltpu.CompilerParams(vmem_limit_bytes=40 * MIB),
        cost_estimate=COST,
        name="attend_back",
    )(
        core, hbm(grad), hbm(queries), hbm(keys), hbm(values), hbm(q_lin), hbm(k_lin), hbm(cosine),
        hbm(sine), q_gain[None, :], k_gain[None, :], *[hbm(p) for p in probs],
        *[hbm(array) for array in before],
    )


def feed_kernel(count, *refs):
    lefts, (wg_ref, wu_ref, dh_ref) = refs[:count], refs[count : count + 3]
    inner_ref, hidden_ref, dg_ref, du_ref = refs[-4:]
    inner = jnp.concatenate([ref[...] for ref in lefts], 0)

    @pl.when(pl.program_id(0) == 0)
    def _():
        inner_ref[...] = inner

    gate = dot_nn(inner, wg_ref[...])
    up = dot_nn(inner, wu_ref[...])
    sig = 1.0 / (1.0 + jnp.exp(-gate))
    silu = gate * sig
    d_hidden = dh_ref[...].astype(jnp.float32)
    hidden_ref[...] = (silu * up).astype(jnp.bfloat16)
    du_ref[...] = (d_hidden * silu).astype(jnp.bfloat16)
    dg_ref[...] = (d_hidden * up * (sig + silu * (1.0 - sig))).astype(jnp.bfloat16)


def feed(first, others, w_gate, w_up, d_hidden, part, before, cols=768):
    lefts = [first, *others]
    rows, width = sum(left.shape[0] for left in lefts), first.shape[1]
    count, units = d_hidden.shape
    here = pl.BlockSpec((rows, width), lambda j: (part, 0))
    block = pl.BlockSpec((rows, cols), lambda j: (part, j))
    weight = pl.BlockSpec((width, cols), lambda j: (0, j))
    out = pltpu.HBM((count, units), jnp.bfloat16)
    return pl.pallas_call(
        functools.partial(feed_kernel, len(lefts)),
        grid=(units // cols,),
        in_specs=[pl.BlockSpec(left.shape, lambda j: (0, 0)) for left in lefts]
        + [weight, weight, block]
        + [pl.BlockSpec(memory_space=pl.ANY)] * len(before),
        out_specs=[here, block, block, block],
        out_shape=[pltpu.HBM((count, width), jnp.bfloat16), out, out, out],
        input_output_aliases={len(lefts) + 3 + i: i for i in range(len(before))},
        compiler_params=pltpu.CompilerParams(vmem_limit_bytes=40 * MIB),
        cost_estimate=COST,
        name="feed",
    )(*lefts, hbm(w_gate), hbm(w_up), hbm(d_hidden), *[hbm(array) for array in before])


ROWS = 128


def wide(ref):
    return ref[...].astype(jnp.float32)


def settle_kernel(core_ref, x_ref, near_ref, far_ref, gain_ref, *refs):
    resid_ref, inner_refs = refs[-1 - BLOCK // ROWS], refs[-(BLOCK // ROWS) :]
    resid = wide(x_ref) + (wide(near_ref) + wide(far_ref))
    resid_ref[...] = resid
    factor = lax.rsqrt(row_mean(resid * resid) + EPS)
    inner = (resid * factor * gain_ref[...]).astype(jnp.bfloat16)
    for j, inner_ref in enumerate(inner_refs):

        @pl.when(pl.program_id(0) == j)
        def _():
            inner_ref[...] = inner


def settle(core, tokens, near, far, gain, part, parts, before):
    rows, width = near.shape
    pieces = rows // ROWS
    block = pl.BlockSpec((ROWS, width), lambda i, core_ref: (i, 0))
    return pl.pallas_call(
        settle_kernel,
        grid_spec=pltpu.PrefetchScalarGridSpec(
            num_scalar_prefetch=1,
            grid=(pieces,),
            in_specs=[
                pl.BlockSpec(
                    (ROWS, width), lambda i, core_ref: ((2 * part + core_ref[0]) * pieces + i, 0)
                ),
                block,
                block,
                pl.BlockSpec((1, width), lambda i, core_ref: (0, 0)),
            ]
            + [pl.BlockSpec(memory_space=pl.ANY)] * len(before),
            out_specs=[pl.BlockSpec((ROWS, width), lambda i, core_ref: (part * pieces + i, 0))]
            + [pl.BlockSpec((ROWS, width), lambda i, core_ref: (0, 0))] * pieces,
        ),
        out_shape=[pltpu.HBM((parts * rows, width), jnp.float32)]
        + [jax.ShapeDtypeStruct((ROWS, width), jnp.bfloat16)] * pieces,
        input_output_aliases={5 + i: i for i in range(len(before))},
        compiler_params=pltpu.CompilerParams(vmem_limit_bytes=24 * MIB),
        cost_estimate=COST,
        name="settle",
    )(core, hbm(tokens), near, far, gain[None, :], *[hbm(array) for array in before])


def half_specs(parts, width):
    steps = BLOCK // ROWS

    def spec(j):
        return pl.BlockSpec(
            (ROWS, width), lambda i, *_: (jnp.clip(i - j * steps, 0, steps - 1), 0)
        )

    return [spec(j) for j in range(parts)]


def put_halves(value, refs):
    for j, ref in enumerate(refs):

        @pl.when(lax.div(pl.program_id(0), BLOCK // ROWS) == j)
        def _():
            ref[...] = value


def norm_grad(near_ref, far_ref, resid_ref, grad_ref, gain_ref):
    resid = resid_ref[...].astype(jnp.float32)
    factor = lax.rsqrt(row_mean(resid * resid) + EPS)
    hat = resid * factor
    d_inner = wide(near_ref) + wide(far_ref)
    both = d_inner * hat
    scaled = d_inner * gain_ref[...]
    back = wide(grad_ref) + factor * (scaled - hat * row_mean(both * gain_ref[...]))
    return back, both


def unsettle_kernel(near_ref, far_ref, resid_ref, grad_ref, gain_ref, out_ref, sum_ref, *low_refs):
    back, both = norm_grad(near_ref, far_ref, resid_ref, grad_ref, gain_ref)
    out_ref[...] = back
    put_halves(back.astype(jnp.bfloat16), low_refs)

    @pl.when(pl.program_id(0) == 0)
    def _():
        sum_ref[...] = jnp.zeros_like(sum_ref)

    sum_ref[0:1, :] += jnp.sum(both, 0, keepdims=True)


def unsettle(far, near, resid, grad, gain):
    rows, width = near.shape
    pieces, parts = BLOCK // ROWS, rows // BLOCK
    block = pl.BlockSpec((ROWS, width), lambda i: (i, 0))
    own = pl.BlockSpec(
        (ROWS, width), lambda i: (2 * pieces * lax.div(i, pieces) + lax.rem(i, pieces), 0)
    )
    return pl.pallas_call(
        unsettle_kernel,
        grid=(rows // ROWS,),
        in_specs=[block, block, block, own, pl.BlockSpec((1, width), lambda i: (0, 0))],
        out_specs=[block, pl.BlockSpec((8, width), lambda i: (0, 0)), *half_specs(parts, width)],
        out_shape=[
            pltpu.HBM((rows, width), jnp.float32),
            jax.ShapeDtypeStruct((8, width), jnp.float32),
        ]
        + [jax.ShapeDtypeStruct((BLOCK, width), jnp.bfloat16)] * parts,
        compiler_params=pltpu.CompilerParams(vmem_limit_bytes=24 * MIB),
        cost_estimate=COST,
        name="unsettle",
    )(near, far, hbm(resid), hbm(grad), gain[None, :])


def last_kernel(core_ref, near_ref, far_ref, x_ref, grad_ref, gain_ref, *out_refs):
    back, _ = norm_grad(near_ref, far_ref, x_ref, grad_ref, gain_ref)
    put_halves(back.astype(jnp.bfloat16), out_refs)


def unsettle_last(core, far, near, tokens, grad, gain):
    rows, width = near.shape
    pieces, parts = BLOCK // ROWS, rows // BLOCK
    block = pl.BlockSpec((ROWS, width), lambda i, core_ref: (i, 0))

    def own(i, core_ref):
        return ((2 * lax.div(i, pieces) + core_ref[0]) * pieces + lax.rem(i, pieces), 0)

    return pl.pallas_call(
        last_kernel,
        grid_spec=pltpu.PrefetchScalarGridSpec(
            num_scalar_prefetch=1,
            grid=(rows // ROWS,),
            in_specs=[
                block, block, pl.BlockSpec((ROWS, width), own), block,
                pl.BlockSpec((1, width), lambda i, core_ref: (0, 0)),
            ],
            out_specs=half_specs(parts, width),
        ),
        out_shape=[jax.ShapeDtypeStruct((BLOCK, width), jnp.bfloat16)] * parts,
        compiler_params=pltpu.CompilerParams(vmem_limit_bytes=24 * MIB),
        cost_estimate=COST,
        name="unsettle_last",
    )(core, near, far, hbm(tokens), hbm(grad), gain[None, :])


def live_rows_kernel(core_ref, value_ref, seg_ref, out_ref):
    out_ref[...] = jnp.where(seg_ref[...] >= 0, value_ref[...].astype(jnp.float32), 0.0).astype(jnp.bfloat16)


def live_rows(core, value, seg_ids):
    count, width = value.shape

    def from_block(i, core_ref):
        return (i ^ core_ref[0], 0)

    return pl.pallas_call(
        live_rows_kernel,
        grid_spec=pltpu.PrefetchScalarGridSpec(
            num_scalar_prefetch=1,
            grid=(count // BLOCK,),
            in_specs=[pl.BlockSpec((BLOCK, width), from_block), pl.BlockSpec((BLOCK, 1), from_block)],
            out_specs=pl.BlockSpec((BLOCK, width), lambda i, core_ref: (i, 0)),
        ),
        out_shape=jax.ShapeDtypeStruct((count, width), jnp.bfloat16),
        compiler_params=pltpu.CompilerParams(vmem_limit_bytes=24 * MIB),
        cost_estimate=COST,
        name="live_rows",
    )(core, hbm(value), seg_ids[:, None])


def ring_of(n):
    order = list(range(0, n, 2)) + [i for i in range(n - 1, 0, -1) if i % 2]
    place = [0] * n
    for spot, index in enumerate(order):
        place[index] = spot
    ahead = tuple((order[i], order[(i + 1) % n]) for i in range(n))
    back = tuple((b, a) for a, b in ahead)
    return order, place, ahead, back


def ring_table(n):
    order, place, _, _ = ring_of(n)
    table = [
        [[order[(place[i] - 1 - s) % n], order[(place[i] + 1 + s) % n]] for s in range(n)]
        for i in range(n)
    ]
    return jnp.asarray(np.array(table, np.int32).reshape(n, 2 * n))[lax.axis_index("dp")]


def ring_first(value_a, value_b, out_a_ref, out_b_ref):
    out_a_ref[...] = value_a.astype(jnp.bfloat16)
    out_b_ref[...] = value_b.astype(jnp.bfloat16)


def ring_last(turned, value_a, value_b, *out_refs):
    rows = value_b.shape[0]
    whole = jnp.concatenate([value_a[:rows], value_b], 1)
    begin = 0
    for flag, ref in zip(turned, out_refs):
        width = ref.shape[0] if flag else ref.shape[1]
        part = whole[:, begin : begin + width]
        ref[...] = part.T if flag else part
        begin += width
    if len(out_refs) > len(turned):
        out_refs[-1][...] = value_a[rows:]


EXTRA = 16


def ring_sum_call(finish, name, step, came, part, extra, out_shape):
    def kernel(*refs):
        came_refs, refs = refs[: len(came)], refs[len(came) :]
        values = [wide(refs[0]), wide(refs[1])]
        if extra:
            rows = refs[2][step * EXTRA : (step + 1) * EXTRA, :].astype(jnp.float32)
            values[0] = jnp.concatenate([values[0], rows], 0)
        if came:
            values = [value + wide(ref) for value, ref in zip(values, came_refs)]
        finish(*values, *refs[2 + len(extra) :])

    vmem = pl.BlockSpec(memory_space=pltpu.VMEM)
    return pl.pallas_call(
        kernel,
        in_specs=[vmem] * (len(came) + 2 + len(extra)),
        out_specs=jax.tree.map(lambda o: vmem, out_shape),
        out_shape=out_shape,
        compiler_params=pltpu.CompilerParams(vmem_limit_bytes=16 * MIB),
        cost_estimate=COST,
        name=name,
    )(*came, *part, *extra)


def ring_call(n, where, step, part, out_shape):
    size, half = part.shape[0] // n, part.shape[1] // 2

    def kernel(where_ref, part_ref, *refs):
        copies = []
        for side, out_ref in enumerate(refs[:2]):
            begin = pl.multiple_of(where_ref[2 * step + side] * size, size)
            copies.append(
                pltpu.make_async_copy(
                    part_ref.at[pl.ds(begin, size), pl.ds(side * half, half)], out_ref, refs[2].at[side]
                )
            )
        for copy in copies:
            copy.start()
        for copy in copies:
            copy.wait()

    return pl.pallas_call(
        kernel,
        in_specs=[pl.BlockSpec(memory_space=pltpu.SMEM), pl.BlockSpec(memory_space=pltpu.HBM)],
        out_specs=[pl.BlockSpec(memory_space=pltpu.VMEM)] * 2,
        out_shape=out_shape,
        scratch_shapes=[pltpu.SemaphoreType.DMA((2,))],
        compiler_params=pltpu.CompilerParams(vmem_limit_bytes=16 * MIB),
        cost_estimate=COST,
        name="ring_piece",
    )(where, hbm(part))


def ring_sides(groups):
    half = sum(right.shape[1] for _, rights in groups for right in rights) // 2
    sides, filled, number = ([], []), 0, 0
    for group, (_, rights) in enumerate(groups):
        for right in rights:
            begin = 0
            while begin < right.shape[1]:
                side = filled // half
                width = min(right.shape[1] - begin, (side + 1) * half - filled)
                sides[side].append((group, number, begin, width))
                begin += width
                filled += width
            number += 1
    return sides, half


def ring_mm_call(n, where, step, groups, out_shape):
    lefts = [left for group, _ in groups for left in group]
    rights = [right for _, group in groups for right in group]
    count = sum(left.shape[0] for left in groups[0][0])
    size = lefts[0].shape[1] // n
    sides, half = ring_sides(groups)
    used = [sorted({term[0] for term in side}) for side in sides]

    def kernel(where_ref, *refs):
        left_refs, refs = refs[: len(lefts)], refs[len(lefts) :]
        right_refs, refs = refs[: len(rights)], refs[len(rights) :]
        out_refs, refs = refs[:2], refs[2:]
        right_bufs, left_bufs, sem = refs[:2], list(refs[2:-1]), refs[-1]
        waits, chunks = ([], []), ({}, {})
        for side in range(2):
            begin = pl.multiple_of(where_ref[2 * step + side] * size, size)
            at = 0
            for group in used[side]:
                buffer = left_bufs.pop(0)
                chunks[side][group] = buffer
                first = sum(len(g[0]) for g in groups[:group])
                row = 0
                for ref in left_refs[first : first + len(groups[group][0])]:
                    rows = ref.shape[0]
                    copy = pltpu.make_async_copy(
                        ref.at[:, pl.ds(begin, size)], buffer.at[pl.ds(row, rows), :], sem.at[side]
                    )
                    copy.start()
                    waits[side].append(copy)
                    row += rows
            for _, number, column, width in sides[side]:
                copy = pltpu.make_async_copy(
                    right_refs[number].at[:, pl.ds(column, width)],
                    right_bufs[side].at[:, pl.ds(at, width)],
                    sem.at[side],
                )
                copy.start()
                waits[side].append(copy)
                at += width
        for side in range(2):
            for copy in waits[side]:
                copy.wait()
            products, at = [], 0
            for group in used[side]:
                width = sum(term[3] for term in sides[side] if term[0] == group)
                products.append(
                    dot_tn(chunks[side][group][...], right_bufs[side][:, at : at + width])
                )
                at += width
            begin = 0
            for product in products:
                width = product.shape[1]
                out_refs[side][:, begin : begin + width] = product.astype(jnp.bfloat16)
                begin += width

    return pl.pallas_call(
        kernel,
        in_specs=[pl.BlockSpec(memory_space=pltpu.SMEM)]
        + [pl.BlockSpec(memory_space=pltpu.HBM)] * (len(lefts) + len(rights)),
        out_specs=[pl.BlockSpec(memory_space=pltpu.VMEM)] * 2,
        out_shape=out_shape,
        scratch_shapes=[pltpu.VMEM((count, half), jnp.bfloat16)] * 2
        + [pltpu.VMEM((count, size), jnp.bfloat16)] * (len(used[0]) + len(used[1]))
        + [pltpu.SemaphoreType.DMA((2,))],
        compiler_params=pltpu.CompilerParams(vmem_limit_bytes=32 * MIB),
        cost_estimate=COST,
        name="ring_piece",
    )(where, *[hbm(i) for i in lefts + rights])


class Order:
    def __init__(self):
        self.last = None

    def run(self, piece, first, *rest):
        if self.last is not None:
            first, _ = lax.optimization_barrier((first, self.last))
        out = piece(first, *rest)
        self.last = jax.tree.leaves(out)[0]
        return out


    def tie(self, value):
        return lax.optimization_barrier((value, self.last))[0]


class Ring:
    def __init__(self, n, where, order, groups, turned, last_shapes):
        self.n, self.where, self.order = n, where, order
        self.last, self.last_shapes = functools.partial(ring_last, turned), [*last_shapes]
        self.step_no, self.parts = -1, []
        _, _, self.ahead, self.back = ring_of(n)
        self.size = groups[0][0][0].shape[1] // n
        self.half = sum(right.shape[1] for _, rights in groups for right in rights) // 2
        self.extra = ()
        if self.size % 128 == 0:
            self.piece, self.source = ring_mm_call, groups
        else:
            (lefts, (first, *others)), *more = groups
            self.piece = ring_call
            self.source = order.run(lambda r: weight_grad([(lefts, [r, *others]), *more]), first)

    def prepare(self):
        step = self.step_no + 1 + len(self.parts)
        if step < self.n:
            shape = jax.ShapeDtypeStruct((self.size, self.half), jnp.bfloat16)
            self.parts.append(
                self.order.run(
                    lambda w: self.piece(self.n, w, step, self.source, [shape] * 2), self.where
                )
            )

    def add(self, extra):
        self.extra = (extra,)
        self.last_shapes.append(jax.ShapeDtypeStruct((EXTRA, self.half), jnp.float32))

    def step(self):
        if self.step_no == self.n - 1:
            return
        if not self.parts:
            self.prepare()
        part = self.parts.pop(0)
        self.step_no += 1
        made = [
            jax.ShapeDtypeStruct((self.size + (EXTRA if self.extra else 0), self.half), jnp.bfloat16),
            jax.ShapeDtypeStruct((self.size, self.half), jnp.bfloat16),
        ]
        if self.step_no == 0 and not self.extra:
            return self.send(part)
        if self.step_no == 0:
            finish, name, out, came = ring_first, "ring_first", made, ()
        elif self.step_no < self.n - 1:
            finish, name, out, came = ring_first, "ring_add", made, self.came
        else:
            finish, name, out, came = self.last, "ring_last", self.last_shapes, self.came
        first, *others = [*came, *part]
        result = self.order.run(
            lambda a: ring_sum_call(
                finish, name, self.step_no, [a, *others][: len(came)], [a, *others][len(came) :],
                self.extra, out,
            ),
            first,
        )
        if self.step_no < self.n - 1:
            self.send(result)
        else:
            self.result = result

    def send(self, held):
        self.came = (lax.ppermute(held[0], "dp", self.ahead), lax.ppermute(held[1], "dp", self.back))


DOTS = {"nn": dot_nn, "nt": dot_nt, "tn": dot_tn}


def pairs_kernel(kind, outs, count, weighed, core_ref, *refs):
    out_refs = refs[-len(outs) - weighed :]
    if weighed:
        sums = jnp.zeros((1, out_refs[-1].shape[1]), jnp.float32)
    for (spots, _), out_ref in zip(outs, out_refs):
        for i, spot in enumerate(spots):
            if spot < 0:
                rows = pl.ds(pl.multiple_of(((-1 - spot) ^ core_ref[0]) * BLOCK, BLOCK), BLOCK)
            else:
                rows = slice(spot * BLOCK, (spot + 1) * BLOCK)
            total = None
            for left_ref, right_ref in zip(refs[: 2 * count : 2], refs[1 : 2 * count : 2]):
                value = DOTS[kind](left_ref[rows, :], right_ref[...])
                total = value if total is None else total + value
            out_ref[i * BLOCK : (i + 1) * BLOCK, :] = total.astype(out_ref.dtype)
            if weighed:
                sums += jnp.sum(total * wide_at(refs[2 * count], rows), 0, keepdims=True)
    if weighed:
        out_refs[-1][...] = jnp.broadcast_to(sums, out_refs[-1].shape)


def wide_at(ref, rows):
    return ref[rows, :].astype(jnp.float32)


def pairs(core, kind, terms, outs, part=0, parts=1, before=(), weights=None, cols=512):
    width = terms[0][1].shape[1 if kind == "nn" else 0]
    steps = width // cols // parts
    begin = part * steps
    ins, specs = [], []
    for left, right in terms:
        ins += [left, right]
        specs.append(pl.BlockSpec(left.shape, lambda j: (0, 0)))
        if kind == "nn":
            specs.append(pl.BlockSpec((right.shape[0], cols), lambda j: (0, begin + j)))
        else:
            specs.append(pl.BlockSpec((cols, right.shape[1]), lambda j: (begin + j, 0)))
    shapes = [(len(o[0]) * BLOCK, o[1]) for o in outs]
    weighed = weights is not None
    if weighed:
        ins.append(weights)
        specs.append(pl.BlockSpec((weights.shape[0], cols), lambda j: (0, begin + j)))
        shapes.append((8, jnp.float32))
    return pl.pallas_call(
        functools.partial(pairs_kernel, kind, outs, len(terms), int(weighed)),
        grid=(steps,),
        in_specs=[pl.BlockSpec(memory_space=pltpu.SMEM)]
        + specs
        + [pl.BlockSpec(memory_space=pl.ANY)] * len(before),
        out_specs=[pl.BlockSpec((rows, cols), lambda j: (0, begin + j)) for rows, _ in shapes],
        out_shape=[pltpu.HBM((rows, width), kind) for rows, kind in shapes],
        input_output_aliases={1 + len(ins) + i: i for i in range(len(before))},
        compiler_params=pltpu.CompilerParams(vmem_limit_bytes=40 * MIB),
        cost_estimate=COST,
        name="pairs",
    )(core, *[hbm(i) for i in ins], *[hbm(array) for array in before])


def split_pair_kernel(core_ref, left_ref, right_ref, mine_ref, *other_refs):
    for spot, own in ((1, False), (0, True)):
        rows = pl.ds(pl.multiple_of((spot ^ core_ref[0]) * BLOCK, BLOCK), BLOCK)
        value = dot_nn(left_ref[rows, :], right_ref[...])
        if own:
            mine_ref[...] = value
        else:
            for j, ref in enumerate(other_refs):
                ref[...] = value[j * ROWS : (j + 1) * ROWS, :].astype(jnp.bfloat16)


def split_pair(core, left, right, cols=512):
    width = right.shape[1]

    def block(rows):
        return pl.BlockSpec((rows, cols), lambda j: (0, j))

    pieces = BLOCK // ROWS
    return pl.pallas_call(
        split_pair_kernel,
        grid=(width // cols,),
        in_specs=[
            pl.BlockSpec(memory_space=pltpu.SMEM),
            pl.BlockSpec(left.shape, lambda j: (0, 0)),
            block(right.shape[0]),
        ],
        out_specs=[block(BLOCK)] + [block(ROWS)] * pieces,
        out_shape=[jax.ShapeDtypeStruct((BLOCK, width), jnp.float32)]
        + [jax.ShapeDtypeStruct((ROWS, width), jnp.bfloat16)] * pieces,
        compiler_params=pltpu.CompilerParams(vmem_limit_bytes=24 * MIB),
        cost_estimate=COST,
        name="split_pair",
    )(core, left, right)


def near_kernel(mine_ref, *refs):
    out_ref = refs[-1]
    for j, came_ref in enumerate(refs[:-1]):

        @pl.when(pl.program_id(0) == j)
        def _():
            out_ref[...] = (mine_ref[...] + wide(came_ref)).astype(jnp.bfloat16)


def near_add(first, others, mine):
    came = [first, *others]
    rows, width = came[0].shape
    block = pl.BlockSpec((rows, width), lambda i: (i, 0))
    return pl.pallas_call(
        near_kernel,
        grid=(len(came),),
        in_specs=[block] + [pl.BlockSpec((rows, width), lambda i: (0, 0))] * len(came),
        out_specs=block,
        out_shape=jax.ShapeDtypeStruct(mine.shape, jnp.bfloat16),
        compiler_params=pltpu.CompilerParams(vmem_limit_bytes=24 * MIB),
        cost_estimate=COST,
        name="near_add",
    )(mine, *came)


def mixed_kernel(resid_ref, near_ref, far_ref, *out_refs):
    total = resid_ref[...] + (wide(near_ref) + wide(far_ref))
    put_halves(total.astype(jnp.bfloat16), out_refs)


def mixed_rows(far, near, resid):
    rows, width = near.shape
    block = pl.BlockSpec((ROWS, width), lambda i: (i, 0))
    return pl.pallas_call(
        mixed_kernel,
        grid=(rows // ROWS,),
        in_specs=[block] * 3,
        out_specs=half_specs(rows // BLOCK, width),
        out_shape=[jax.ShapeDtypeStruct((BLOCK, width), jnp.bfloat16)] * (rows // BLOCK),
        compiler_params=pltpu.CompilerParams(vmem_limit_bytes=24 * MIB),
        cost_estimate=COST,
        name="mixed",
    )(hbm(resid), near, far)


def nt_kernel(*refs):
    out_ref = refs[-1]
    begin = 0
    for left_ref in refs[1:-1]:
        rows = slice(begin, begin + left_ref.shape[0])
        out_ref[rows, :] = dot_nt(left_ref[...], refs[0][...]).astype(jnp.bfloat16)
        begin += left_ref.shape[0]


def times_turned(lefts, right, cols=512):
    rows = sum(left.shape[0] for left in lefts)
    return pl.pallas_call(
        nt_kernel,
        grid=(right.shape[0] // cols,),
        in_specs=[pl.BlockSpec((cols, right.shape[1]), lambda j: (j, 0))]
        + [pl.BlockSpec(left.shape, lambda j: (0, 0)) for left in lefts],
        out_specs=pl.BlockSpec((rows, cols), lambda j: (0, j)),
        out_shape=pltpu.HBM((rows, right.shape[0]), jnp.bfloat16),
        compiler_params=pltpu.CompilerParams(vmem_limit_bytes=40 * MIB),
        cost_estimate=COST,
        name="times_turned",
    )(hbm(right), *lefts)


def weight_grad_kernel(counts, *refs):
    out_ref = refs[-1]
    at, begin = 0, 0
    for lefts, rights in counts:
        left = refs[at][...]
        if lefts > 1:
            left = jnp.concatenate([ref[...] for ref in refs[at : at + lefts]], 0)
        for ref in refs[at + lefts : at + lefts + rights]:
            width = ref.shape[1]
            out_ref[:, begin : begin + width] = dot_tn(left, ref[...]).astype(jnp.bfloat16)
            begin += width
        at += lefts + rights


def weight_grad(groups, rows=256):
    width = groups[0][0][0].shape[1]
    ins, specs, cols = [], [], 0
    for lefts, rights in groups:
        ins += [*lefts, *rights]
        specs += [pl.BlockSpec((left.shape[0], rows), lambda i: (0, i)) for left in lefts]
        specs += [pl.BlockSpec(right.shape, lambda i: (0, 0)) for right in rights]
        cols += sum(right.shape[1] for right in rights)
    return pl.pallas_call(
        functools.partial(weight_grad_kernel, [(len(a), len(b)) for a, b in groups]),
        grid=(width // rows,),
        in_specs=specs,
        out_specs=pl.BlockSpec((rows, cols), lambda i: (i, 0)),
        out_shape=jax.ShapeDtypeStruct((width, cols), jnp.bfloat16),
        compiler_params=pltpu.CompilerParams(vmem_limit_bytes=32 * MIB),
        cost_estimate=COST,
        name="weight_grad",
    )(*[hbm(i) for i in ins])


def join_kernel(core_ref, *refs):
    for i, ref in enumerate(refs[:-1]):

        @pl.when(pl.program_id(0) == i)
        def _():
            refs[-1][...] = ref[...]


def join(first, others, core, mine):
    blocks = [block for pair in zip(mine, [first, *others]) for block in pair]
    width = first.shape[1]
    return pl.pallas_call(
        join_kernel,
        grid_spec=pltpu.PrefetchScalarGridSpec(
            num_scalar_prefetch=1,
            grid=(len(blocks),),
            in_specs=[pl.BlockSpec((BLOCK, width), lambda i, core_ref: (0, 0))] * len(blocks),
            out_specs=pl.BlockSpec((BLOCK, width), lambda i, core_ref: (i ^ core_ref[0], 0)),
        ),
        out_shape=jax.ShapeDtypeStruct((BLOCK * len(blocks), width), first.dtype),
        compiler_params=pltpu.CompilerParams(vmem_limit_bytes=24 * MIB),
        cost_estimate=COST,
        name="join",
    )(core, *blocks)


def to_core(value):
    return lax.ppermute(value, "tensor", CORE_SWAP)


def to_chip(value):
    return lax.ppermute(value, "tensor", CHIP_SWAP)


def low(value):
    return value.astype(jnp.bfloat16)


def on_device(
    n, tokens, seg_ids, cotangent, attn_gain, w_query, w_key, w_value, w_out, mlp_gain, w_gate, w_up,
    w_down, query_gain, key_gain,
):
    count, width = tokens.shape
    size = query_gain.shape[0]
    parts = 2
    rows = count // parts
    core_no = lax.axis_index("tensor") % 2
    core = core_no.astype(jnp.int32)[None]
    where = ring_table(n)
    order = Order()
    run = order.run

    index = jnp.arange(count, dtype=jnp.int32)
    place = jnp.where(seg_ids >= 0, index - seg_ids, index).astype(jnp.float32)
    freq = THETA ** (-(jnp.arange(size // 2, dtype=jnp.float32) * 2.0) / size)
    turn = place[:, None] * freq[None, :]
    cosine, sine = jnp.cos(turn), jnp.sin(turn)
    cosine, sine = jnp.concatenate([cosine, cosine], -1), jnp.concatenate([-sine, sine], -1)

    normed, queries, keys, values, q_lin, k_lin = run(
        front, tokens, attn_gain, w_query, w_key, w_value, cosine, sine, query_gain, key_gain
    )
    wide_low = (jnp.float32, jnp.bfloat16)

    def mine_other(mine, other):
        return ((mine, wide_low[0]), *[((block,), wide_low[1]) for block in other])

    attended, probs, near, far = [], [], [], []
    for j in range(parts):
        out = run(lambda q: attend(q, keys, values, seg_ids, j, parts), queries)
        attended.append(out[0])
        probs += out[1:]
        mine, *other = run(lambda a: split_pair(core, a, w_out), out[0])
        other = [to_core(piece) for piece in other]
        near.append(run(near_add, other[0], other[1:], mine))
        far.append(to_chip(near[j]))

    grad_low = run(lambda c: live_rows(core, c, seg_ids), cotangent)
    grad_low, where = lax.optimization_barrier((grad_low, where))
    d_hidden = run(lambda g: times_turned([g], w_down), grad_low)
    resid, fed = (), ()
    for j in range(parts):
        held, *inner_own = run(
            lambda f: settle(core, tokens, near[j], f, mlp_gain, j, parts, resid), far[j]
        )
        resid = (held,)
        inner_other = [to_core(piece) for piece in inner_own]
        fed = run(
            lambda o: feed(inner_own[0], [*inner_own[1:], o, *inner_other[1:]], w_gate, w_up, d_hidden, j, fed),
            inner_other[0],
        )
    inner, hidden, d_gate, d_up = fed

    def shape(*extent):
        return jax.ShapeDtypeStruct(extent, jnp.float32)

    units, share = w_gate.shape[1], width // n
    q_cols, k_cols = w_query.shape[1], w_key.shape[1]
    (resid,) = resid
    both = mine_other((0, 2), (1, 3))
    turns = where[::2, None] == jnp.arange(n)[None, :]
    made, came = {}, {}

    def send(name):
        values = made[name]
        if name in TIES:
            values = order.tie(values)
        came[name] = [lax.ppermute(value, "tensor", SENDS[name]) for value in values]

    def run_came(piece, name, *rest):
        first, *others = came[name]
        return run(piece, first, others, *rest)

    mlp_ring = Ring(
        n, where, order, [([grad_low], [hidden]), ([inner], [d_gate, d_up])], (True, False, False),
        [shape(units, share), shape(share, units), shape(share, units)],
    )
    rings = {"mlp": mlp_ring}

    def ring_piece(name):
        return lambda: rings[name].prepare()

    def ring_step(name):
        return lambda: rings[name].step()

    def mlp_first():
        mlp_ring.prepare()
        mlp_ring.step()

    def inner_first():
        made["d_inner"] = run(
            lambda d: pairs(core, "nt", [(d, w_gate), (d_up, w_up)], both, 0, 2, ()), d_gate
        )

    def inner_second():
        made["d_inner"], *made["core3"] = run(
            lambda d: pairs(core, "nt", [(d, w_gate), (d_up, w_up)], both, 1, 2, made["d_inner"]), d_gate
        )

    def inner_near():
        made["x3"] = [run_came(near_add, "core3", made["d_inner"])]

    def mixed_products():
        made["mixed"], *made["core2"] = run(lambda h: pairs(core, "nn", [(h, w_down)], both), hidden)

    def mixed_near():
        made["x2"] = [run_came(near_add, "core2", made["mixed"])]

    def mixed_sum():
        made["coreM"] = run(mixed_rows, came["x2"][0], made["x2"][0], resid)

    def mixed_join():
        made["mixed"] = run_came(join, "coreM", core, made["coreM"])

    def resid_grad():
        made["d_resid"], made["mlp_sums"], *made["coreB"] = run(
            unsettle, came["x3"][0], made["x3"][0], resid, grad_low, mlp_gain
        )

    def attended_order():
        blocks = [part[i : i + BLOCK] for part in attended for i in range(0, rows, BLOCK)]

        def swap(first):
            turned = [blocks[i ^ 1] for i in range(len(blocks))]
            return jnp.where(
                core_no == 0, jnp.concatenate([first, *blocks[1:]], 0), jnp.concatenate(turned, 0)
            )

        made["attended"] = run(swap, blocks[0])

    def attended_grad():
        made["d_branch"] = [b for pair in zip(made["coreB"], came["coreB"]) for b in pair]
        made["d_attended"] = run(
            lambda d: times_turned([*made["d_branch"][:-1], d], w_out), made["d_branch"][-1]
        )
        made["d_lin"], made["head_sums"] = (), 0.0

    def heads_grad(g):
        def piece():
            *made["d_lin"], total = run(
                lambda a: attend_back(
                    core, a, queries, keys, values, q_lin, k_lin, cosine, sine, query_gain, key_gain,
                    probs, g, made["d_lin"],
                ),
                made["d_attended"],
            )
            made["head_sums"] = made["head_sums"] + total

        return piece

    def normed_grad():
        d_q_lin, d_k_lin, d_values = made["d_lin"]
        rings["lin"] = Ring(
            n, where, order, [(made["d_branch"], [made["attended"]]), ([normed], made["d_lin"])],
            (True, False, False, False),
            [shape(q_cols, share), shape(share, q_cols), shape(share, k_cols), shape(share, k_cols)],
        )
        made["d_normed"], *made["core4"], attn_sums = run(
            lambda d: pairs(
                core, "nt", [(d, w_query), (d_k_lin, w_key), (d_values, w_value)],
                mine_other((-1, -3), (-2, -4)), weights=normed,
            ),
            d_q_lin,
        )
        head_sums = made["head_sums"]
        gains = [0.5 * made["mlp_sums"][0], attn_sums[0] / attn_gain, head_sums[0], head_sums[1]]
        made["gains1"] = [jnp.concatenate([part.reshape(n, -1) for part in gains], 1)]

    def gains_core():
        made["gains2"] = [run_came(lambda f, o: f + made["gains1"][0], "gains1")]

    def gains_chip():
        def in_turn(came, others):
            total = jnp.sum(jnp.where(turns[:, :, None], (came + made["gains2"][0])[None], 0.0), 1)
            spare = EXTRA * rings["lin"].half - total.shape[1]
            return jnp.pad(low(total), ((0, 0), (0, spare))).reshape(n * EXTRA, -1)

        rings["lin"].add(run_came(in_turn, "gains2"))

    def normed_near():
        made["x4"] = [run_came(near_add, "core4", made["d_normed"])]

    def tokens_grad():
        made["coreG"] = run(
            lambda f: unsettle_last(core, f, made["x4"][0], tokens, made["d_resid"], attn_gain),
            came["x4"][0],
        )

    def tokens_join():
        made["tokens"] = run_came(join, "coreG", core, made["coreG"])

    pieces = {
        "piece0": mlp_first, "piece": ring_piece("mlp"), "add": ring_step("mlp"),
        "dih0": inner_first, "dih1": inner_second, "near3": inner_near,
        "sel": attended_order, "mixp": mixed_products, "near2": mixed_near, "mixed": mixed_sum, "joinM": mixed_join,
        "unsettle": resid_grad, "datt": attended_grad, "att0": heads_grad(0), "att1": heads_grad(1),
        "dn": normed_grad, "gc": gains_core, "gx": gains_chip, "near4": normed_near,
        "ul": tokens_grad, "joinG": tokens_join,
        "lp": ring_piece("lin"), "lf": ring_step("lin"), "la": ring_step("lin"),
    }
    producers = {
        "core3": "dih1", "x3": "near3", "core2": "mixp", "x2": "near2", "coreM": "mixed",
        "coreB": "unsettle", "gains1": "dn", "gains2": "gc", "core4": "dn", "x4": "near4", "coreG": "ul",
    }
    counts = {}
    for step in SCHEDULE:
        pieces[step]()
        counts[step] = counts.get(step, 0) + 1
        for name, producer in producers.items():
            if TIES.get(name, (producer, 1)) == (step, counts[step]):
                send(name)
    for ring in rings.values():
        while ring.step_no < n - 1:
            ring.step()
    mixed, grad_tokens = made["mixed"], made["tokens"]
    grad_down, grad_gate, grad_up = mlp_ring.result
    grad_out, grad_query, grad_key, grad_value, extra = rings["lin"].result
    gains, begins = extra.reshape(-1), np.cumsum([0, width, width, size, size]) // n
    mlp_sum, attn_sum, q_sum, k_sum = [gains[begins[i] : begins[i + 1]] for i in range(4)]
    return (
        mixed,
        grad_tokens,
        attn_sum,
        grad_query,
        grad_key,
        grad_value,
        grad_out,
        mlp_sum,
        grad_gate,
        grad_up,
        grad_down,
        q_sum,
        k_sum,
    )


def solution(mesh):
    rows, cols = P("dp", "tensor"), P("tensor", "dp")
    return jax.shard_map(
        functools.partial(on_device, mesh.shape["dp"]),
        mesh=mesh,
        in_specs=(
            P("dp", None), P("dp"), P("dp", None), P(), P(None, "tensor"), P(None, "tensor"),
            P(None, "tensor"), P("tensor", None), P(), P(None, "tensor"), P(None, "tensor"),
            P("tensor", None), P(), P(),
        ),
        out_specs=(
            P("dp", None), P("dp", None), P("dp"), rows, rows, rows, cols, P("dp"), rows, rows, cols,
            P("dp"), P("dp"),
        ),
        check_vma=False,
    )
```
